256 devices in a mesh: sec: 256 (over y, x, z, core).
Axes of the slice: x: 4, y: 4, z: 8, core: 2. Of those that a mesh axis runs over, the one named last changes fastest.
Arguments:
- front_reflect: float32 [256, 384, 384], P('sec'), may hold values from -0.125 to 0.125
- front_through: float32 [256, 384, 384], P('sec'), may hold values from -1 to 1
- back_reflect: float32 [256, 384, 384], P('sec'), may hold values from -0.125 to 0.125
- back_through: float32 [256, 384, 384], P('sec'), may hold values from -1 to 1
- depth_maps: float32 [256, 4, 384, 384], P('sec'), may hold values from -1 to 1
- incident: float32 [384, 128], replicated, may hold values from -6 to 6
Outputs:
- through_field: float32 [256, 384, 128], P('sec')
- reflected: float32 [256, 384, 128], P('sec')
- depth_fields: float32 [256, 4, 384, 128], P('sec')
The draws below stay inside these ranges and needn't reach their ends.
All inputs are finite; a program needn't handle non-finite values.
Results may differ from the reference program's by a relative error of at most 0.00013.
Values sent between devices are 32-bit elements; how exact they have to be, the bound alone decides.
A program may use at most 64 MiB of HBM per device.

```python
import math
import jax
import jax.numpy as jnp
from jax import lax

M = 384
INC = 128
NEU = 3
SEGMENTS = 3
DEPTHS = 4
SECTIONS = 256
STRIDE = 32


def near_identity(key, extent):
    noise_key = jax.random.fold_in(key, 0)
    entries = jax.random.truncated_normal(noise_key, -2.0, 2.0, extent, jnp.float32)
    centre = jnp.full(extent[:-1] + (1,), 0.8, jnp.float32)
    identity = jnp.eye(M, dtype=jnp.float32)
    return centre * identity + 0.4 * entries / math.sqrt(M)


def draw_front_through(key, part):
    return near_identity(jax.random.fold_in(key, 101), (SECTIONS, M, M))


def draw_back_through(key, part):
    return near_identity(jax.random.fold_in(key, 202), (SECTIONS, M, M))


def draw_depth_maps(key, part):
    return near_identity(jax.random.fold_in(key, 303), (SECTIONS, DEPTHS, M, M))


def shard_levels(own_key, dims, shards, low, top_value):
    def one(position, shards_of):
        steps = jax.random.uniform(jax.random.fold_in(jax.random.fold_in(own_key, 6), position), (shards_of,), jnp.float32, low / len(shards), top_value / len(shards))
        return jnp.repeat(jnp.exp(steps), dims[position] // shards_of).reshape((-1,) + (1,) * (len(dims) - position - 1))

    gain = one(*shards[0])
    for cut in shards[1:]:
        gain = gain * one(*cut)
    return gain


def scatter_about(own_key, shape, width, most, cuts=(), kind=jnp.bfloat16):
    level = shard_levels(own_key, shape, cuts, -0.22, 0.18) if cuts else 1.0
    array = jax.random.normal(own_key, shape, jnp.float32) * width * level
    return jnp.minimum(jnp.maximum(array, -most), most).astype(kind)


def setup_inputs(seed: int = 0) -> dict:
    key_of = jax.random.split(jax.random.key(seed), 7)
    front_reflect = scatter_about(key_of[0], (SECTIONS, M, M), (5 * M) ** -0.5, 0.125, ((0, 256),), jnp.float32)
    front_through = draw_front_through(jax.random.fold_in(key_of[6], 71), 0)
    back_reflect = scatter_about(key_of[2], (SECTIONS, M, M), (5 * M) ** -0.5, 0.125, ((0, 256),), jnp.float32)
    back_through = draw_back_through(jax.random.fold_in(key_of[6], 71), 0)
    depth_maps = draw_depth_maps(jax.random.fold_in(key_of[6], 71), 0)
    incident = scatter_about(key_of[5], (M, INC), 1.0, 6.0, (), jnp.float32)
    return dict(front_reflect=front_reflect, front_through=front_through, back_reflect=back_reflect, back_through=back_through, depth_maps=depth_maps, incident=incident)


def product(former, latter):
    return jnp.matmul(former, latter, precision=lax.Precision.HIGHEST)


def series(bounce, identity):
    total = identity + bounce
    for _ in range(NEU - 1):
        total = identity + product(bounce, total)
    return total


def combine(upper, lower):
    upper_reflect, upper_through, upper_mirror, upper_return = upper
    lower_reflect, lower_through, lower_mirror, lower_return = lower
    identity = jnp.eye(M, dtype=jnp.float32)
    forward_sum = series(product(upper_mirror, lower_reflect), identity)
    reverse_sum = series(product(lower_reflect, upper_mirror), identity)
    g_through = product(forward_sum, upper_through)
    new_through = product(lower_through, g_through)
    new_reflect = upper_reflect + product(upper_return, product(lower_reflect, g_through))
    h_return = product(reverse_sum, lower_return)
    new_return = product(upper_return, h_return)
    new_mirror = lower_mirror + product(lower_through, product(upper_mirror, h_return))
    return (new_reflect, new_through, new_mirror, new_return)


def reference(front_reflect, front_through, back_reflect, back_through, depth_maps, incident):
    identity = jnp.eye(M, dtype=jnp.float32)
    current = (front_reflect, front_through, back_reflect, back_through)
    for level_index in range(SEGMENTS):
        distance = STRIDE * 2 ** level_index
        zeros = jnp.zeros((distance, M, M), jnp.float32)
        ones = jnp.broadcast_to(identity, (distance, M, M))
        upper = (
            jnp.concatenate([zeros, current[0][:-distance]], axis=0),
            jnp.concatenate([ones, current[1][:-distance]], axis=0),
            jnp.concatenate([zeros, current[2][:-distance]], axis=0),
            jnp.concatenate([ones, current[3][:-distance]], axis=0),
        )
        current = combine(upper, current)
    through_field = product(current[1], incident)
    reflected = product(current[0], incident)
    entering = jnp.concatenate([incident[None], through_field[:-1]], axis=0)
    depth_fields = jnp.einsum("sjmn,snc->sjmc", depth_maps, entering, precision=lax.Precision.HIGHEST)
    return (through_field, reflected, depth_fields)
```

```python
import jax
import jax.numpy as jnp
from jax import lax
from jax.sharding import PartitionSpec as P

SEGMENTS = 3


def passed_along(value, axis, by):
    length = lax.axis_size(axis)
    pairs = [(i, i + by) for i in range(length) if 0 <= i + by < length]
    return lax.ppermute(value, axis, pairs)


def product(former, latter):
    return jnp.dot(
        former, latter, precision=lax.Precision.HIGH, preferred_element_type=jnp.float32
    )


def series(bounce, identity):
    partial_value = identity + bounce
    partial_value = identity + product(bounce, partial_value)
    return (partial_value, identity + product(bounce, partial_value))


def combine(upper, lower, complete):
    upper_reflect, upper_through, upper_mirror, upper_return = upper
    lower_reflect, lower_through, lower_mirror, lower_return = lower
    identity = jnp.eye(lower_reflect.shape[0], dtype=jnp.float32)
    partial_value, forward_sum = series(product(upper_mirror, lower_reflect), identity)
    g_through = product(forward_sum, upper_through)
    new_through = product(lower_through, g_through)
    new_reflect = upper_reflect + product(upper_return, product(lower_reflect, g_through))
    if not complete:
        return (new_reflect, new_through)
    reverse_sum = series(product(lower_reflect, upper_mirror), identity)[1]
    h_return = product(reverse_sum, lower_return)
    new_return = product(upper_return, h_return)
    new_mirror = lower_mirror + product(lower_through, product(upper_mirror, h_return))
    return (new_reflect, new_through, new_mirror, new_return)


def restore(arrived, missing, identity):
    return (
        arrived[0],
        arrived[1] + missing * identity,
        arrived[2],
        arrived[3] + missing * identity,
    )


def per_device(front_reflect, front_through, back_reflect, back_through, depth_maps, incident):
    stride = lax.axis_size("sec") // 2**SEGMENTS
    position = lax.axis_index("sec")
    identity = jnp.eye(front_reflect.shape[1], dtype=jnp.float32)
    current = (front_reflect[0], front_through[0], back_reflect[0], back_through[0])
    for level_index in range(SEGMENTS - 1):
        distance = stride * 2**level_index
        arrived = passed_along(current, "sec", distance)
        missing = jnp.where(position >= distance, 0.0, 1.0)
        current = combine(restore(arrived, missing, identity), current, True)
    distance = stride * 2 ** (SEGMENTS - 1)
    missing = jnp.where(position >= distance, 0.0, 1.0)
    arrived = passed_along(current, "sec", distance)
    final_reflect, final_through = combine(restore(arrived, missing, identity), current, False)
    through_field = product(final_through, incident)
    reflected = product(final_reflect, incident)
    entering = passed_along(through_field, "sec", 1)
    first_section = jnp.where(position == 0, 1.0, 0.0)
    entering = entering + first_section * incident
    depth_fields = jnp.einsum(
        "jmn,nc->jmc",
        depth_maps[0],
        entering,
        precision=lax.Precision.HIGH,
        preferred_element_type=jnp.float32,
    )
    return (through_field[None], reflected[None], depth_fields[None])


def solution(mesh):
    in_specs = (
        P("sec", None, None),
        P("sec", None, None),
        P("sec", None, None),
        P("sec", None, None),
        P("sec", None, None, None),
        P(),
    )
    out_specs = (P("sec", None, None), P("sec", None, None), P("sec", None, None, None))
    return jax.shard_map(
        per_device, mesh=mesh, in_specs=in_specs, out_specs=out_specs, check_vma=False
    )
```

```python
import functools

import jax
import jax.numpy as jnp
from jax import lax
from jax.experimental import pallas as pl
from jax.experimental.pallas import tpu as pltpu
from jax.sharding import PartitionSpec as P


F32, BF16 = jnp.float32, jnp.bfloat16
MESH = pl.DeviceIdType.MESH
M, INC, DEPTHS = 384, 128, 4

FQ, FR, FT, FU, LQ, LR, LT, LU = range(8)
CQ, CR, CT, CU = range(8, 12)
DQ, DR, DT, DU, R6, T6 = range(12, 18)
HQ, HU, RIN, ROUT, POUT, R23, Q01, U01, T3, P3, TX, TM, TRP = range(18, 31)
BLOCKS = 31
HT, HR, T01, R01, G2, P1, RB, RC, TA, TB, PL, GL, TL, RL, ENT = range(15)
VECS = 15


def halves(x):
    high = x.astype(BF16)
    return high, (x - high.astype(F32)).astype(BF16)


def left(x):
    high, low = halves(x)
    return jnp.concatenate([high, low, high], axis=1)


def right(x):
    high, low = halves(x)
    return jnp.concatenate([high, high, low], axis=0)


def mm(a, b):
    return jnp.dot(left(a), right(b), preferred_element_type=F32)


def spread(mirror, reflect):
    bounce = mm(mirror, reflect)
    return bounce, bounce + mm(bounce, bounce)


def summed(bounce, both, value):
    partial_value = value + mm(both, value)
    return partial_value, value + mm(bounce, partial_value)


def forward(former, latter_reflect):
    mirror, reflect, through, back = former
    bounce, both = spread(mirror, latter_reflect)
    g_through = summed(bounce, both, through)[1]
    return reflect + mm(back, mm(latter_reflect, g_through)), g_through


def applied(mirror, back, field, reflected, latter_reflect):
    bounce = mm(mirror, latter_reflect)
    value = field
    for _ in range(3):
        value = field + mm(bounce, value)
    return value, reflected + mm(back, mm(latter_reflect, value))


def joined(mirror, back, field, reflected, latter):
    own_mirror, own_reflect, own_through, own_back = latter
    cut = field.shape[1]
    bounce, both = spread(mirror, own_reflect)
    value = jnp.concatenate([field, mm(mirror, own_back)], axis=1)
    partial_value, full_value = summed(bounce, both, value)
    through = mm(own_through, full_value)
    turned = mm(own_reflect, jnp.concatenate([full_value[:, :cut], partial_value[:, cut:]], axis=1))
    returned = mm(back, jnp.concatenate([turned[:, :cut], own_back + turned[:, cut:]], axis=1))
    return (
        through[:, :cut],
        reflected + returned[:, :cut],
        own_mirror + through[:, cut:],
        returned[:, cut:],
    )


def index_of(x, y, z, c):
    return ((y * 4 + x) * 8 + z) * 2 + c


def middle_x(x, c):
    return lax.rem(x + jnp.where(x // 2 == c, 1, 3), 4)


def producer(k_half, y, middle, z):
    at = jnp.where(y == 0, 0, jnp.where(y == 1, k_half, jnp.where(y == 2, 2, 2 + k_half)))
    return index_of(middle, at, z, 1 - k_half)


def kernel(
    reflect_ref, through_ref, mirror_ref, back_ref, maps_ref, incident_ref,
    through_out, reflected_out, depth_out,
    W, V, maps, maps_left, depth, send, recv, local,
):
    me = lax.axis_index("sec")
    c, z, x, y = me % 2, (me // 2) % 8, (me // 16) % 4, me // 64
    x_half = x // 2
    middle = middle_x(x, c)
    base = 1 - x % 2
    group_c = jnp.where(x % 2 == 1, x_half, 1 - x_half)
    residue = base * 16 + z * 2 + group_c
    chain_half = 1 - c

    def col(at_y, at_c):
        return index_of(x, at_y, z, at_c)

    def home(at_y, half):
        return index_of(base + 2 * half, at_y, z, group_c)

    is_a = c == 0
    is_mid = is_a | (y == 0) | (y == 2)
    is_hub = (is_a & (y == 1)) | ((c == 1) & (y == 0))
    is_two = y == 2
    is_a0, is_a2, is_a3 = is_a & (y == 0), is_a & (y == 2), is_a & (y == 3)
    is_b0, is_b2 = (c == 1) & (y == 0), (c == 1) & (y == 2)
    is_last = is_a3 | is_b2
    is_first_home = (x_half == 0) & (y == 0)

    barrier = pltpu.get_barrier_semaphore()

    def greet(condition, device):
        @pl.when(condition)
        def _():
            pl.semaphore_signal(barrier, inc=1, device_id=(device,), device_id_type=MESH)

    def count(condition, n=1):
        return jnp.where(condition, n, 0)

    greet(is_a, home(y, 0))
    greet(is_a, home(y, 1))
    expected = 1
    greet(is_b0 | is_b2, col(y // 2 + 1, 0))
    expected += count(is_a & ((y == 1) | (y == 2)))
    greet(is_b0 | is_b2, col(y // 2, 0))
    expected += count(is_a & (y < 2))
    greet(is_b0, home(0, 0))
    expected += count(is_first_home)
    greet(is_b2, col(3, 0))
    expected += count(is_a3)
    greet(is_a & (y == 1), col(0, 0))
    expected += count(is_a0)
    greet(is_a & ((y == 1) | (y == 2)), col(y + 1, 0))
    greet(is_b0, col(2, 1))
    expected += count((is_a & (y >= 2)) | is_b2)
    greet(is_two, col(1 - c, c))
    expected += count(is_hub)
    greet(is_a3, col(1, 0))
    expected += count(is_a & (y == 1))
    greet(is_a3, col(2, 0))
    expected += count(is_a2)
    greet((y == 0) & (x_half == 1), index_of(middle, 0, z, 0))
    expected += count(is_a0)
    greet(y >= 1, index_of(middle, x_half, z, 1 - x_half))
    expected += count(is_hub, 3)
    greet(y >= 2, producer(x_half, y, middle, z))
    expected += count(is_two) + count(is_last)
    before = jnp.maximum(me - 1, 0)
    bc, bz, bx, by = before % 2, (before // 2) % 8, (before // 16) % 4, before // 64
    first_before = (by == 0) & (bx // 2 == 0)
    greet(
        me >= 1,
        jnp.where(first_before, before, producer(bx // 2, by, middle_x(bx, bc), bz)),
    )
    goes_on = ~(is_a3 & (residue == 31))
    expected += count(is_first_home) + count(is_a0) + count(is_hub) + count(is_two)
    expected += count(is_last & goes_on)

    maps_copy = pltpu.make_async_copy(maps_ref.at[0], maps, local.at[0])
    maps_copy.start()

    @pl.when(is_first_home)
    def _():
        pltpu.make_async_copy(through_ref.at[0], W.at[T3], local.at[1]).start()
        pltpu.make_async_copy(reflect_ref.at[0], W.at[P3], local.at[2]).start()

    pl.semaphore_wait(barrier, expected)

    other = lax.rem(me + 1, lax.axis_size("sec"))

    def message(source, target, s, r, device):
        return pltpu.make_async_remote_copy(
            src_ref=source, dst_ref=target, send_sem=send.at[s], recv_sem=recv.at[r],
            device_id=(device,), device_id_type=MESH,
        )

    finals = []

    def post(condition, source, target, s, r, device):
        @pl.when(condition)
        def _():
            message(source, target, s, r, device).start()

        finals.append((condition, source, s))

    def got(target, r):
        message(target, target, 0, r, other).wait_recv()

    def sent(source, s):
        message(source, source, s, 0, other).wait_send()

    sections = (mirror_ref, reflect_ref, through_ref, back_ref)
    middle_a = index_of(middle, y, z, 0)

    def first_send(part):
        message(
            sections[part].at[0], W.at[4 * x_half + part], part, 4 * x_half + part, middle_a
        ).start()

    def pass_on(part):
        @pl.when(is_a)
        def _():
            got(W.at[FQ + part], FQ + part)
            got(W.at[LQ + part], LQ + part)

        post(is_a & ((y == 1) | (y == 2)), W.at[FQ + part], W.at[LQ + part], 4 + part, LQ + part,
             col(2 * (y - 1), 1))
        post(is_a & (y < 2), W.at[LQ + part], W.at[FQ + part], 8 + part, FQ + part, col(2 * y, 1))
        post(is_a2, W.at[LQ + part], W.at[DQ + part], 8 + part, 8 + part, col(2, 1))
        if part in (0, 3):
            at = 0 if part == 0 else 1
            post(is_a0, W.at[FQ + part], W.at[HQ + at], 4 + part, 14 + at, col(0, 1))
        else:
            post(is_a3, W.at[FQ + part], W.at[R6 + part - 1], 4 + part, 12 + part - 1, col(2, 1))

    first_send(0)
    first_send(1)

    @pl.when(is_first_home)
    def _():
        pltpu.make_async_copy(through_ref.at[0], W.at[T3], local.at[1]).wait()
        pltpu.make_async_copy(reflect_ref.at[0], W.at[P3], local.at[2]).wait()
        V[TL] = mm(W[T3], incident_ref[...])
        V[RL] = mm(W[P3], incident_ref[...])

    post(is_first_home, V.at[TL], V.at[HT], 28, 16, index_of(middle, 0, z, 1))
    post(is_first_home, V.at[RL], V.at[HR], 29, 17, index_of(middle, 0, z, 1))
    post(is_first_home, V.at[TL], V.at[ENT], 30, 25, other)

    maps_copy.wait()
    for j in range(DEPTHS):
        maps_left[j * M : (j + 1) * M, :] = left(maps[j])

    pass_on(0)
    sent(sections[0].at[0], 0)
    first_send(2)
    pass_on(1)
    sent(sections[1].at[0], 1)
    first_send(3)

    @pl.when(is_mid)
    def _():
        @pl.when(c == 1)
        def _():
            for part in (0, 1):
                got(W.at[FQ + part], FQ + part)
                got(W.at[LQ + part], LQ + part)

        bounce, both = spread(W[FQ], W[LR])
        W[TX] = bounce
        W[TM] = both

    pass_on(2)

    @pl.when(is_mid)
    def _():
        @pl.when(c == 1)
        def _():
            got(W.at[FT], FT)
            got(W.at[LT], LT)

        g_through = summed(W[TX], W[TM], W[FT])[1]
        W[CT] = mm(W[LT], g_through)
        W[TRP] = mm(W[LR], g_through)

    pass_on(3)

    @pl.when(is_b2)
    def _():
        for part in range(4):
            got(W.at[DQ + part], 8 + part)
        got(W.at[R6], 12)
        got(W.at[T6], 13)
        W[RIN], W[P3] = forward((W[DQ], W[DR], W[DT], W[DU]), W[R6])

    @pl.when(is_mid)
    def _():
        @pl.when(c == 1)
        def _():
            got(W.at[FU], FU)
            got(W.at[LU], LU)

        W[CR] = W[FR] + mm(W[FU], W[TRP])

    post((is_a & (y >= 2)) | is_b2, W.at[CR], W.at[RIN], 16, 18,
         jnp.where(is_a, col(y - 1, 0), col(0, 1)))

    @pl.when(is_mid)
    def _():
        bounce = W[TX]
        mirrored = mm(W[FQ], W[LU])
        partial_value, full_value = summed(bounce, W[TM], mirrored)
        W[CQ] = W[LQ] + mm(W[LT], full_value)
        W[CU] = mm(W[FU], W[LU] + mm(W[LR], partial_value))

    @pl.when(is_a0)
    def _():
        V[T01] = mm(W[CT], incident_ref[...])
        V[R01] = mm(W[CR], incident_ref[...])

    post(is_a0, V.at[T01], V.at[HT], 14, 16, col(1, 0))
    post(is_a0, W.at[CQ], W.at[HQ], 12, 14, col(1, 0))
    post(is_a0, V.at[R01], V.at[HR], 15, 17, col(1, 0))
    post(is_a0, W.at[CU], W.at[HU], 13, 15, col(1, 0))
    post(is_a0, V.at[T01], V.at[TL], 21, 23, home(0, 1))
    post(is_a0, V.at[R01], V.at[RL], 23, 24, home(0, 1))
    post(is_a0, V.at[T01], V.at[ENT], 22, 25, 32 + residue + 1)

    def turn(step, carry):
        @pl.when((is_hub | is_two) & (step == 2 * c))
        def _():
            @pl.when(~is_b2)
            def _():
                got(W.at[RIN], 18)

            W[ROUT], W[POUT] = forward((W[CQ], W[CR], W[CT], W[CU]), W[RIN])

            @pl.when(is_two)
            def _():
                message(W.at[ROUT], W.at[R23], 17, 19, col(1 - c, c)).start()

            @pl.when(is_a2)
            def _():
                message(W.at[POUT], W.at[POUT], 18, 20, col(3, 0)).start()

        @pl.when(is_hub & (step == 1))
        def _():
            got(V.at[HT], 16)
            got(W.at[HQ], 14)
            got(V.at[HR], 17)
            got(W.at[HU], 15)
            V[T01], V[R01], W[Q01], W[U01] = joined(
                W[HQ], W[HU], V[HT], V[HR], (W[CQ], W[CR], W[CT], W[CU])
            )
            message(V.at[T01], V.at[TL], 21, 23, home(1, chain_half)).start()
            message(V.at[R01], V.at[RL], 23, 24, home(1, chain_half)).start()
            message(V.at[T01], V.at[ENT], 22, 25, 32 * (2 + chain_half) + residue + 1).start()

        return carry

    lax.fori_loop(0, 3, turn, 0)
    finals.append((is_two, W.at[ROUT], 17))
    finals.append((is_a2, W.at[POUT], 18))
    finals.append((is_hub, V.at[T01], 21))
    finals.append((is_hub, V.at[R01], 23))
    finals.append((is_hub, V.at[T01], 22))

    @pl.when(is_b2)
    def _():
        W[T3] = mm(W[T6], W[P3])

    @pl.when(is_hub)
    def _():
        got(W.at[R23], 19)
        V[G2], V[RC] = applied(W[Q01], W[U01], V[T01], V[R01], W[R23])
        value, V[RB] = applied(W[HQ], W[HU], V[HT], V[HR], W[ROUT])
        V[P1] = mm(W[POUT], value)

    post(is_hub, V.at[G2], V.at[GL], 20, 22, jnp.where(is_a, col(3, 0), col(2, 1)))
    post(is_hub, V.at[P1], V.at[PL], 19, 21, col(2, c))
    post(is_hub, V.at[RC], V.at[RL], 25, 24, home(3, chain_half))
    post(is_hub, V.at[RB], V.at[RL], 24, 24, home(2, chain_half))

    @pl.when(is_last)
    def _():
        got(V.at[GL], 22)

        @pl.when(is_a3)
        def _():
            got(W.at[POUT], 20)

        value = mm(W[POUT], V[GL])
        V[TB] = mm(W[jnp.where(is_a, CT, T3)], value)

    post(is_last, V.at[TB], V.at[TL], 26, 23, home(3, chain_half))
    post(is_last & goes_on, V.at[TB], V.at[ENT], 27, 25, 32 * (6 + chain_half) + residue + 1)

    @pl.when(is_two)
    def _():
        got(V.at[PL], 21)
        V[TA] = mm(W[CT], V[PL])

    post(is_two, V.at[TA], V.at[TL], 21, 23, home(2, chain_half))
    post(is_two, V.at[TA], V.at[ENT], 22, 25, 32 * (4 + chain_half) + residue + 1)

    @pl.when(~is_first_home)
    def _():
        got(V.at[TL], 23)
        got(V.at[RL], 24)

    through_copy = pltpu.make_async_copy(V.at[TL], through_out.at[0], local.at[3])
    reflected_copy = pltpu.make_async_copy(V.at[RL], reflected_out.at[0], local.at[4])
    through_copy.start()
    reflected_copy.start()

    @pl.when(me >= 1)
    def _():
        got(V.at[ENT], 25)

    @pl.when(me == 0)
    def _():
        V[ENT] = incident_ref[...]

    depth[...] = jnp.dot(maps_left[...], right(V[ENT]), preferred_element_type=F32).reshape(
        DEPTHS, M, INC
    )
    depth_copy = pltpu.make_async_copy(depth, depth_out.at[0], local.at[5])
    depth_copy.start()

    sent(sections[2].at[0], 2)
    sent(sections[3].at[0], 3)
    for condition, source, s in finals:
        @pl.when(condition)
        def _(source=source, s=s):
            sent(source, s)

    through_copy.wait()
    reflected_copy.wait()
    depth_copy.wait()


def per_device(front_reflect, front_through, back_reflect, back_through, depth_maps, incident):
    anywhere = pl.BlockSpec(memory_space=pl.ANY)
    return pl.pallas_call(
        kernel,
        out_shape=(
            jax.ShapeDtypeStruct((1, M, INC), F32),
            jax.ShapeDtypeStruct((1, M, INC), F32),
            jax.ShapeDtypeStruct((1, DEPTHS, M, INC), F32),
        ),
        in_specs=[anywhere] * 5 + [pl.BlockSpec(memory_space=pltpu.VMEM)],
        out_specs=(anywhere,) * 3,
        scratch_shapes=[
            pltpu.VMEM((BLOCKS, M, M), F32),
            pltpu.VMEM((VECS, M, INC), F32),
            pltpu.VMEM((DEPTHS, M, M), F32),
            pltpu.VMEM((DEPTHS * M, 3 * M), BF16),
            pltpu.VMEM((DEPTHS, M, INC), F32),
            pltpu.SemaphoreType.DMA((31,)),
            pltpu.SemaphoreType.DMA((26,)),
            pltpu.SemaphoreType.DMA((6,)),
        ],
        compiler_params=pltpu.CompilerParams(
            collective_id=0, has_side_effects=True, vmem_limit_bytes=56 * 2**20
        ),
        name="chains",
    )(front_reflect, front_through, back_reflect, back_through, depth_maps, incident)


def solution(mesh):
    in_specs = (
        P("sec", None, None),
        P("sec", None, None),
        P("sec", None, None),
        P("sec", None, None),
        P("sec", None, None, None),
        P(),
    )
    out_specs = (P("sec", None, None), P("sec", None, None), P("sec", None, None, None))
    return jax.shard_map(
        per_device, mesh=mesh, in_specs=in_specs, out_specs=out_specs, check_vma=False
    )
```

```python
import functools

import jax
import jax.numpy as jnp
from jax import lax
from jax.experimental import pallas as pl
from jax.experimental.pallas import tpu as pltpu
from jax.sharding import PartitionSpec as P


F32, BF16 = jnp.float32, jnp.bfloat16
MESH = pl.DeviceIdType.MESH
M, INC, DEPTHS = 384, 128, 4

FQ, FR, FT, FU, LQ, LR, LT, LU = range(8)
CQ, CR, CT, CU = range(8, 12)
DQ, DR, DT, DU, R6, T6 = range(12, 18)
HQ, HU, RIN, ROUT, POUT, R23, Q01, U01, T3, P3, TX, TM, TRP = range(18, 31)
BLOCKS = 31
HT, HR, T01, R01, G2, P1, RB, RC, TA, TB, PL, GL, TL, RL, ENT = range(15)
VECS = 15


def halves(x):
    high = x.astype(BF16)
    return high, (x - high.astype(F32)).astype(BF16)


def left(x):
    high, low = halves(x)
    return jnp.concatenate([high, low, high], axis=1)


def right(x):
    high, low = halves(x)
    return jnp.concatenate([high, high, low], axis=0)


def mm(a, b):
    return jnp.dot(left(a), right(b), preferred_element_type=F32)


def spread(mirror, reflect):
    bounce = mm(mirror, reflect)
    return bounce, bounce + mm(bounce, bounce)


def summed(bounce, both, value):
    partial_value = value + mm(both, value)
    return partial_value, value + mm(bounce, partial_value)


def forward(former, latter_reflect):
    mirror, reflect, through, back = former
    bounce, both = spread(mirror, latter_reflect)
    g_through = summed(bounce, both, through)[1]
    return reflect + mm(back, mm(latter_reflect, g_through)), g_through


def applied(mirror, back, field, reflected, latter_reflect):
    bounce = mm(mirror, latter_reflect)
    value = field
    for _ in range(3):
        value = field + mm(bounce, value)
    return value, reflected + mm(back, mm(latter_reflect, value))


def joined(mirror, back, field, reflected, latter):
    own_mirror, own_reflect, own_through, own_back = latter
    cut = field.shape[1]
    bounce, both = spread(mirror, own_reflect)
    value = jnp.concatenate([field, mm(mirror, own_back)], axis=1)
    partial_value, full_value = summed(bounce, both, value)
    through = mm(own_through, full_value)
    turned = mm(own_reflect, jnp.concatenate([full_value[:, :cut], partial_value[:, cut:]], axis=1))
    returned = mm(back, jnp.concatenate([turned[:, :cut], own_back + turned[:, cut:]], axis=1))
    return (
        through[:, :cut],
        reflected + returned[:, :cut],
        own_mirror + through[:, cut:],
        returned[:, cut:],
    )


def index_of(x, y, z, c):
    return ((y * 4 + x) * 8 + z) * 2 + c


def middle_x(x, c):
    return lax.rem(x + jnp.where(x // 2 == c, 1, 3), 4)


def producer(k_half, y, middle, z):
    at = jnp.where(y == 3, 2 + k_half, y)
    return index_of(middle, at, z, 1 - k_half)


def kernel(
    reflect_ref, through_ref, mirror_ref, back_ref, incident_ref,
    through_out, reflected_out, entering_out,
    W, V, send, recv, local,
):
    me = lax.axis_index("sec")
    c, z, x, y = me % 2, (me // 2) % 8, (me // 16) % 4, me // 64
    x_half = x // 2
    middle = middle_x(x, c)
    base = 1 - x % 2
    group_c = jnp.where(x % 2 == 1, x_half, 1 - x_half)
    residue = base * 16 + z * 2 + group_c
    chain_half = 1 - c

    def col(at_y, at_c):
        return index_of(x, at_y, z, at_c)

    def home(at_y, half):
        return index_of(base + 2 * half, at_y, z, group_c)

    is_a = c == 0
    is_mid = is_a | (y == 0) | (y == 2)
    is_hub = (is_a & (y == 1)) | ((c == 1) & (y == 0))
    is_two = y == 2
    is_a0, is_a2, is_a3 = is_a & (y == 0), is_a & (y == 2), is_a & (y == 3)
    is_b0, is_b2 = (c == 1) & (y == 0), (c == 1) & (y == 2)
    is_a1, is_b1 = is_a & (y == 1), (c == 1) & (y == 1)
    is_last = is_a3 | is_b2
    is_first_home = (x_half == 0) & (y == 0)

    barrier = pltpu.get_barrier_semaphore()

    def greet(condition, device):
        @pl.when(condition)
        def _():
            pl.semaphore_signal(barrier, inc=1, device_id=(device,), device_id_type=MESH)

    def count(condition, n=1):
        return jnp.where(condition, n, 0)

    greet(is_a, home(y, 0))
    greet(is_a, home(y, 1))
    expected = 1
    greet(is_b0 | is_b2, col(y // 2 + 1, 0))
    expected += count(is_a & ((y == 1) | (y == 2)))
    greet(is_b0 | is_b2, col(y // 2, 0))
    expected += count(is_a & (y < 2))
    greet(is_b0, home(0, 0))
    expected += count(is_first_home)
    greet(is_b2, col(3, 0))
    expected += count(is_a3)
    greet(y == 1, col(0, c))
    expected += count(is_a0)
    greet(is_a & ((y == 1) | (y == 2)), col(y + 1, 0))
    greet(is_b0, col(2, 1))
    expected += count((is_a & (y >= 2)) | is_b2)
    greet(is_two, col(1 - c, c))
    expected += count(is_hub)
    greet(is_a3, col(1, 0))
    expected += count(is_a1)
    greet(is_a3, col(2, 0))
    expected += count(is_a2)
    greet((y == 0) & (x_half == 1), index_of(middle, 0, z, 0))
    expected += count(is_a0)
    greet((y >= 2) | ((y == 1) & (x_half == 1)), index_of(middle, x_half, z, 1 - x_half))
    expected += count(is_hub, 3)
    greet((y == 1) & (x_half == 0), index_of(middle, 1, z, 1))
    expected += count(is_b1)
    greet(y >= 2, producer(x_half, y, middle, z))
    expected += count(is_two) + count(is_last)
    before = jnp.maximum(me - 1, 0)
    bc, bz, bx, by = before % 2, (before // 2) % 8, (before // 16) % 4, before // 64
    first_before = (by == 0) & (bx // 2 == 0)
    greet(
        me >= 1,
        jnp.where(first_before, before, producer(bx // 2, by, middle_x(bx, bc), bz)),
    )
    goes_on = ~(is_a3 & (residue == 31))
    expected += count(is_first_home) + count(is_a0) + count(y == 1) + count(is_two)
    expected += count(is_last & goes_on)

    @pl.when(is_first_home)
    def _():
        pltpu.make_async_copy(through_ref.at[0], W.at[T3], local.at[1]).start()
        pltpu.make_async_copy(reflect_ref.at[0], W.at[P3], local.at[2]).start()

    pl.semaphore_wait(barrier, expected)

    other = lax.rem(me + 1, lax.axis_size("sec"))

    def message(source, target, s, r, device):
        return pltpu.make_async_remote_copy(
            src_ref=source, dst_ref=target, send_sem=send.at[s], recv_sem=recv.at[r],
            device_id=(device,), device_id_type=MESH,
        )

    finals = []

    def post(condition, source, target, s, r, device):
        @pl.when(condition)
        def _():
            message(source, target, s, r, device).start()

        finals.append((condition, source, s))

    def got(target, r):
        message(target, target, 0, r, other).wait_recv()

    def sent(source, s):
        message(source, source, s, 0, other).wait_send()

    sections = (mirror_ref, reflect_ref, through_ref, back_ref)
    middle_a = index_of(middle, y, z, 0)

    def rows(block, half):
        return W.at[block, pl.ds(half * (M // 2), M // 2)]

    def piece(part, half):
        return sections[part].at[0, pl.ds(half * (M // 2), M // 2)]

    def slot(block, half):
        return 2 * block + half

    def first_send(part, half):
        message(
            piece(part, half), rows(4 * x_half + part, half), 2 * part + half,
            slot(4 * x_half + part, half), middle_a,
        ).start()

    def turned(third):
        return (3, 2) if third else (2, 3)

    def later_send(order, half):
        @pl.when(y == 0)
        def _():
            first_send(turned(order == 2)[0], half)

        @pl.when(y > 0)
        def _():
            first_send(order, half)

    def pass_on(part, half, who):
        @pl.when(who)
        def _():
            got(rows(FQ + part, half), slot(FQ + part, half))
            got(rows(LQ + part, half), slot(LQ + part, half))

        at = 8 + 2 * part + half
        post(who & ((y == 1) | (y == 2)), rows(FQ + part, half), rows(LQ + part, half), at,
             slot(LQ + part, half), col(2 * (y - 1), 1))
        post(who & (y < 2), rows(LQ + part, half), rows(FQ + part, half), at + 8,
             slot(FQ + part, half), col(2 * y, 1))
        post(who & (y == 2), rows(LQ + part, half), rows(DQ + part, half), at + 8,
             slot(8 + part, half), col(2, 1))
        if part in (0, 3):
            first = 0 if part == 0 else 1
            post(who & (y == 0), rows(FQ + part, half), rows(HQ + first, half), at,
                 slot(14 + first, half), col(0, 1))
        else:
            post(who & (y == 3), rows(FQ + part, half), rows(R6 + part - 1, half), at,
                 slot(12 + part - 1, half), col(2, 1))

    def both_halves(block, receive):
        for half in (0, 1):
            got(rows(block, half), slot(receive, half))

    for part in (0, 1):
        for half in (0, 1):
            first_send(part, half)

    @pl.when(is_first_home)
    def _():
        pltpu.make_async_copy(through_ref.at[0], W.at[T3], local.at[1]).wait()
        pltpu.make_async_copy(reflect_ref.at[0], W.at[P3], local.at[2]).wait()
        V[TL] = mm(W[T3], incident_ref[...])
        V[RL] = mm(W[P3], incident_ref[...])

    post(is_first_home, V.at[TL], V.at[HT], 40, 36, index_of(middle, 0, z, 1))
    post(is_first_home, V.at[RL], V.at[HR], 41, 37, index_of(middle, 0, z, 1))
    post(is_first_home, V.at[TL], V.at[ENT], 42, 45, other)

    for part in (0, 1):
        for half in (0, 1):
            pass_on(part, half, is_a)
            sent(piece(part, half), 2 * part + half)
            later_send(part + 2, half)

    @pl.when(is_mid)
    def _():
        @pl.when(c == 1)
        def _():
            for part in (0, 1):
                both_halves(FQ + part, FQ + part)
                both_halves(LQ + part, LQ + part)

        bounce, both = spread(W[FQ], W[LR])
        W[TX] = bounce
        W[TM] = both

    for half in (0, 1):
        pass_on(2, half, is_a & (y > 0))
        pass_on(3, half, is_a0)

    @pl.when(is_a0)
    def _():
        partial_value, full_value = summed(W[TX], W[TM], mm(W[FQ], W[LU]))
        W[TRP] = full_value
        W[CU] = mm(W[FU], W[LU] + mm(W[LR], partial_value))

    post(is_a0, W.at[CU], W.at[HU], 27, 35, col(1, 0))

    @pl.when(is_mid & ~is_a0)
    def _():
        @pl.when(c == 1)
        def _():
            both_halves(FT, FT)
            both_halves(LT, LT)

        g_through = summed(W[TX], W[TM], W[FT])[1]
        W[CT] = mm(W[LT], g_through)
        W[TRP] = mm(W[LR], g_through)

    for half in (0, 1):
        pass_on(3, half, is_a & (y > 0))
        pass_on(2, half, is_a0)

    @pl.when(is_a0)
    def _():
        W[CQ] = W[LQ] + mm(W[LT], W[TRP])

    post(is_a0, W.at[CQ], W.at[HQ], 26, 34, col(1, 0))

    @pl.when(is_a0)
    def _():
        value = summed(W[TX], W[TM], mm(W[FT], incident_ref[...]))[1]
        V[T01] = mm(W[LT], value)
        V[R01] = mm(W[FR], incident_ref[...]) + mm(W[FU], mm(W[LR], value))

    @pl.when(is_b2)
    def _():
        for part in range(4):
            both_halves(DQ + part, 8 + part)
        both_halves(R6, 12)
        both_halves(T6, 13)
        W[RIN], W[P3] = forward((W[DQ], W[DR], W[DT], W[DU]), W[R6])

    @pl.when(is_mid & ~is_a0)
    def _():
        @pl.when(c == 1)
        def _():
            both_halves(FU, FU)
            both_halves(LU, LU)

        W[CR] = W[FR] + mm(W[FU], W[TRP])

    post((is_a & (y >= 2)) | is_b2, W.at[CR], W.at[RIN], 24, 38,
         jnp.where(is_a, col(y - 1, 0), col(0, 1)))

    @pl.when(is_mid & ~is_a0)
    def _():
        partial_value, full_value = summed(W[TX], W[TM], mm(W[FQ], W[LU]))
        W[CQ] = W[LQ] + mm(W[LT], full_value)
        W[CU] = mm(W[FU], W[LU] + mm(W[LR], partial_value))

    post(is_a0, V.at[T01], V.at[HT], 28, 36, col(1, 0))
    post(is_a0, V.at[R01], V.at[HR], 29, 37, col(1, 0))
    post(is_a0, V.at[pl.ds(T01, 2)], V.at[pl.ds(TL, 2)], 30, 43, home(0, 1))
    post(is_a0, V.at[T01], V.at[ENT], 31, 45, 32 + residue + 1)

    def turn(step, carry):
        @pl.when((is_hub | is_two) & (step == 2 * c))
        def _():
            @pl.when(~is_b2)
            def _():
                got(W.at[RIN], 38)

            W[ROUT], W[POUT] = forward((W[CQ], W[CR], W[CT], W[CU]), W[RIN])

            @pl.when(is_two)
            def _():
                message(W.at[ROUT], W.at[R23], 25, 39, col(1 - c, c)).start()

            @pl.when(is_a2)
            def _():
                message(W.at[POUT], W.at[POUT], 32, 40, col(3, 0)).start()

        @pl.when(is_hub & (step == 1))
        def _():
            got(V.at[HT], 36)
            got(V.at[HR], 37)

            @pl.when(is_a)
            def _():
                got(W.at[HQ], 34)
                got(W.at[HU], 35)

            @pl.when(c == 1)
            def _():
                both_halves(HQ, 14)
                both_halves(HU, 15)

            V[T01], V[R01], W[Q01], W[U01] = joined(
                W[HQ], W[HU], V[HT], V[HR], (W[CQ], W[CR], W[CT], W[CU])
            )

            @pl.when(is_a)
            def _():
                message(V.at[pl.ds(T01, 2)], V.at[pl.ds(TL, 2)], 30, 43, home(1, 1)).start()
                message(V.at[T01], V.at[ENT], 31, 45, 32 * 3 + residue + 1).start()

            @pl.when(c == 1)
            def _():
                message(V.at[pl.ds(T01, 2)], V.at[pl.ds(T01, 2)], 30, 46, col(1, 1)).start()

        return carry

    lax.fori_loop(0, 3, turn, 0)
    finals.append((is_two, W.at[ROUT], 25))
    finals.append((is_a2, W.at[POUT], 32))
    finals.append((is_hub, V.at[pl.ds(T01, 2)], 30))
    finals.append((is_a1, V.at[T01], 31))

    @pl.when(is_b1)
    def _():
        got(V.at[pl.ds(T01, 2)], 46)

    post(is_b1, V.at[pl.ds(T01, 2)], V.at[pl.ds(TL, 2)], 30, 43, home(1, 0))
    post(is_b1, V.at[T01], V.at[ENT], 31, 45, 32 * 2 + residue + 1)

    @pl.when(is_b2)
    def _():
        W[T3] = mm(W[T6], W[P3])

    @pl.when(is_hub)
    def _():
        got(W.at[R23], 39)
        V[G2], V[RC] = applied(W[Q01], W[U01], V[T01], V[R01], W[R23])
        value, V[RB] = applied(W[HQ], W[HU], V[HT], V[HR], W[ROUT])
        V[P1] = mm(W[POUT], value)

    post(is_hub, V.at[G2], V.at[GL], 33, 42, jnp.where(is_a, col(3, 0), col(2, 1)))
    post(is_hub, V.at[P1], V.at[PL], 34, 41, col(2, c))
    post(is_hub, V.at[RC], V.at[RL], 35, 44, home(3, chain_half))
    post(is_hub, V.at[RB], V.at[RL], 36, 44, home(2, chain_half))

    @pl.when(is_last)
    def _():
        got(V.at[GL], 42)

        @pl.when(is_a3)
        def _():
            got(W.at[POUT], 40)

        value = mm(W[POUT], V[GL])
        V[TB] = mm(W[jnp.where(is_a, CT, T3)], value)

    post(is_last, V.at[TB], V.at[TL], 37, 43, home(3, chain_half))
    post(is_last & goes_on, V.at[TB], V.at[ENT], 38, 45, 32 * (6 + chain_half) + residue + 1)

    @pl.when(is_two)
    def _():
        got(V.at[PL], 41)
        V[TA] = mm(W[CT], V[PL])

    post(is_two, V.at[TA], V.at[TL], 30, 43, home(2, chain_half))
    post(is_two, V.at[TA], V.at[ENT], 31, 45, 32 * (4 + chain_half) + residue + 1)

    @pl.when((y < 2) & ~is_first_home)
    def _():
        got(V.at[pl.ds(TL, 2)], 43)

    @pl.when(y >= 2)
    def _():
        got(V.at[TL], 43)
        got(V.at[RL], 44)

    through_copy = pltpu.make_async_copy(V.at[TL], through_out, local.at[3])
    reflected_copy = pltpu.make_async_copy(V.at[RL], reflected_out, local.at[4])
    through_copy.start()
    reflected_copy.start()

    @pl.when(me >= 1)
    def _():
        got(V.at[ENT], 45)

    @pl.when(me == 0)
    def _():
        V[ENT] = incident_ref[...]

    entering_copy = pltpu.make_async_copy(V.at[ENT], entering_out, local.at[5])
    entering_copy.start()

    for part in (2, 3):
        for half in (0, 1):
            sent(piece(part, half), 2 * part + half)
    for condition, source, s in finals:
        @pl.when(condition)
        def _(source=source, s=s):
            sent(source, s)

    through_copy.wait()
    reflected_copy.wait()
    entering_copy.wait()


def fields_kernel(through_ref, reflected_ref, entering_ref, maps_ref,
                  through_out, reflected_out, depth_out):
    @pl.when(pl.program_id(0) == 0)
    def _():
        through_out[0] = through_ref[...]
        reflected_out[0] = reflected_ref[...]

    depth_out[0, 0] = mm(maps_ref[0, 0], entering_ref[...])


def per_device(front_reflect, front_through, back_reflect, back_through, depth_maps, incident):
    anywhere = pl.BlockSpec(memory_space=pl.ANY)
    field = jax.ShapeDtypeStruct((M, INC), F32)
    through, reflected, entering = pl.pallas_call(
        kernel,
        out_shape=(field,) * 3,
        in_specs=[pl.BlockSpec(memory_space=pltpu.HBM)] * 4 + [pl.BlockSpec(memory_space=pltpu.VMEM)],
        out_specs=(anywhere,) * 3,
        scratch_shapes=[
            pltpu.VMEM((BLOCKS, M, M), F32),
            pltpu.VMEM((VECS, M, INC), F32),
            pltpu.SemaphoreType.DMA((43,)),
            pltpu.SemaphoreType.DMA((47,)),
            pltpu.SemaphoreType.DMA((6,)),
        ],
        compiler_params=pltpu.CompilerParams(
            collective_id=0, has_side_effects=True, vmem_limit_bytes=44 * 2**20
        ),
        name="chains",
    )(front_reflect, front_through, back_reflect, back_through, incident)
    whole = pl.BlockSpec((M, INC), lambda j: (0, 0))
    out = pl.BlockSpec((1, M, INC), lambda j: (0, 0, 0))
    return pl.pallas_call(
        fields_kernel,
        grid=(DEPTHS,),
        out_shape=(
            jax.ShapeDtypeStruct((1, M, INC), F32),
            jax.ShapeDtypeStruct((1, M, INC), F32),
            jax.ShapeDtypeStruct((1, DEPTHS, M, INC), F32),
        ),
        in_specs=[whole, whole, whole, pl.BlockSpec((1, 1, M, M), lambda j: (0, j, 0, 0))],
        out_specs=(out, out, pl.BlockSpec((1, 1, M, INC), lambda j: (0, j, 0, 0))),
        name="depths",
    )(through, reflected, entering, depth_maps)


def solution(mesh):
    in_specs = (
        P("sec", None, None),
        P("sec", None, None),
        P("sec", None, None),
        P("sec", None, None),
        P("sec", None, None, None),
        P(),
    )
    out_specs = (P("sec", None, None), P("sec", None, None), P("sec", None, None, None))
    return jax.shard_map(
        per_device, mesh=mesh, in_specs=in_specs, out_specs=out_specs, check_vma=False
    )
```

```python
import functools

import jax
import jax.numpy as jnp
from jax import lax
from jax.experimental import pallas as pl
from jax.experimental.pallas import tpu as pltpu
from jax.sharding import PartitionSpec as P


F32, BF16 = jnp.float32, jnp.bfloat16
MESH = pl.DeviceIdType.MESH
M, INC, DEPTHS = 384, 128, 4

FQ, FR, FT, FU, LQ, LR, LT, LU = range(8)
CQ, CR, CT, CU = range(8, 12)
DQ, DR, DT, DU, R6, T6 = range(12, 18)
HQ, HU, RIN, ROUT, POUT, R23, Q01, U01, T3, P3, TX, TM, TRP = range(18, 31)
BLOCKS = 31
HT, HR, T01, R01, G2, G3, P1, RB, RC, TA, TB, PL, GL, TL, RL, ENT = range(16)
VECS = 16


def halves(x):
    high = x.astype(BF16)
    return high, (x - high.astype(F32)).astype(BF16)


def left(x):
    high, low = halves(x)
    return jnp.concatenate([high, low, high], axis=1)


def right(x):
    high, low = halves(x)
    return jnp.concatenate([high, high, low], axis=0)


def mm(a, b):
    return jnp.dot(left(a), right(b), preferred_element_type=F32)


def spread(mirror, reflect):
    bounce = mm(mirror, reflect)
    return bounce, bounce + mm(bounce, bounce)


def summed(bounce, both, value):
    partial_value = value + mm(both, value)
    return partial_value, value + mm(bounce, partial_value)


def forward(former, latter_reflect):
    mirror, reflect, through, back = former
    bounce, both = spread(mirror, latter_reflect)
    g_through = summed(bounce, both, through)[1]
    return reflect + mm(back, mm(latter_reflect, g_through)), g_through


def bounced(bounce, field):
    value = field
    for _ in range(3):
        value = field + mm(bounce, value)
    return value


def joined(mirror, back, field, reflected, latter):
    own_mirror, own_reflect, own_through, own_back = latter
    cut = field.shape[1]
    bounce, both = spread(mirror, own_reflect)
    value = jnp.concatenate([field, mm(mirror, own_back)], axis=1)
    partial_value, full_value = summed(bounce, both, value)
    through = mm(own_through, full_value)
    turned = mm(own_reflect, jnp.concatenate([full_value[:, :cut], partial_value[:, cut:]], axis=1))
    returned = mm(back, jnp.concatenate([turned[:, :cut], own_back + turned[:, cut:]], axis=1))
    return (
        through[:, :cut],
        reflected + returned[:, :cut],
        own_mirror + through[:, cut:],
        returned[:, cut:],
    )


def index_of(x, y, z, c):
    return ((y * 4 + x) * 8 + z) * 2 + c


def middle_x(x, c):
    return lax.rem(x + jnp.where(x // 2 == c, 1, 3), 4)


def producer(k_half, y, middle, z):
    at = jnp.where(y == 3, 2 + k_half, y)
    return index_of(middle, at, z, 1 - k_half)


def kernel(
    reflect_ref, through_ref, mirror_ref, back_ref, maps_ref, incident_ref,
    through_out, reflected_out, depth_out,
    W, V, maps, maps_left, depth, send, recv, local,
):
    me = lax.axis_index("sec")
    c, z, x, y = me % 2, (me // 2) % 8, (me // 16) % 4, me // 64
    x_half = x // 2
    middle = middle_x(x, c)
    base = 1 - x % 2
    group_c = jnp.where(x % 2 == 1, x_half, 1 - x_half)
    residue = base * 16 + z * 2 + group_c
    chain_half = 1 - c

    def col(at_y, at_c):
        return index_of(x, at_y, z, at_c)

    def home(at_y, half):
        return index_of(base + 2 * half, at_y, z, group_c)

    is_a = c == 0
    is_mid = is_a | (y == 0) | (y == 2)
    is_hub = (is_a & (y == 1)) | ((c == 1) & (y == 0))
    is_two = y == 2
    is_a0, is_a2, is_a3 = is_a & (y == 0), is_a & (y == 2), is_a & (y == 3)
    is_b0, is_b2 = (c == 1) & (y == 0), (c == 1) & (y == 2)
    is_a1, is_b1 = is_a & (y == 1), (c == 1) & (y == 1)
    is_b3 = (c == 1) & (y == 3)
    is_last = is_a3 | is_b2
    is_first_home = (x_half == 0) & (y == 0)

    barrier = pltpu.get_barrier_semaphore()

    def greet(condition, device):
        @pl.when(condition)
        def _():
            pl.semaphore_signal(barrier, inc=1, device_id=(device,), device_id_type=MESH)

    def count(condition, n=1):
        return jnp.where(condition, n, 0)

    greet(is_a, home(y, 0))
    greet(is_a, home(y, 1))
    expected = 1
    greet(is_b0 | is_b2, col(y // 2 + 1, 0))
    expected += count(is_a & ((y == 1) | (y == 2)))
    greet(is_b0 | is_b2, col(y // 2, 0))
    expected += count(is_a & (y < 2))
    greet(is_b0, home(0, 0))
    expected += count(is_first_home)
    greet(is_b2, col(3, 0))
    expected += count(is_a3)
    greet(y == 1, col(0, c))
    expected += count(is_a0)
    greet(is_a & ((y == 1) | (y == 2)), col(y + 1, 0))
    greet(is_b0, col(2, 1))
    expected += count((is_a & (y >= 2)) | is_b2)
    greet(is_b3, col(2, 1))
    expected += count(is_b2)
    greet(is_b0, col(3, 1))
    expected += count(is_b3)
    greet(is_two, col(1 - c, c))
    expected += count(is_hub)
    greet(is_a3, col(1, 0))
    expected += count(is_a1)
    greet(is_a3, col(2, 0))
    expected += count(is_a2)
    greet((y == 0) & (x_half == 1), index_of(middle, 0, z, 0))
    expected += count(is_a0)
    greet((y >= 2) | ((y == 1) & (x_half == 1)), index_of(middle, x_half, z, 1 - x_half))
    expected += count(is_hub, 3)
    greet((y == 1) & (x_half == 0), index_of(middle, 1, z, 1))
    expected += count(is_b1)
    greet(y >= 2, producer(x_half, y, middle, z))
    expected += count(is_two) + count(is_last)
    before = jnp.maximum(me - 1, 0)
    bc, bz, bx, by = before % 2, (before // 2) % 8, (before // 16) % 4, before // 64
    first_before = (by == 0) & (bx // 2 == 0)
    greet(
        me >= 1,
        jnp.where(first_before, before, producer(bx // 2, by, middle_x(bx, bc), bz)),
    )
    goes_on = ~(is_a3 & (residue == 31))
    expected += count(is_first_home) + count(is_a0) + count(y == 1) + count(is_two)
    expected += count(is_last & goes_on)

    @pl.when(is_first_home)
    def _():
        pltpu.make_async_copy(through_ref.at[0], W.at[T3], local.at[1]).start()
        pltpu.make_async_copy(reflect_ref.at[0], W.at[P3], local.at[2]).start()

    maps_copy = pltpu.make_async_copy(maps_ref.at[0], maps, local.at[0])
    maps_copy.start()
    pl.semaphore_wait(barrier, expected)

    other = lax.rem(me + 1, lax.axis_size("sec"))

    def message(source, target, s, r, device):
        return pltpu.make_async_remote_copy(
            src_ref=source, dst_ref=target, send_sem=send.at[s], recv_sem=recv.at[r],
            device_id=(device,), device_id_type=MESH,
        )

    finals = []

    def post(condition, source, target, s, r, device):
        @pl.when(condition)
        def _():
            message(source, target, s, r, device).start()

        finals.append((condition, source, s))

    def got(target, r):
        message(target, target, 0, r, other).wait_recv()

    def sent(source, s):
        message(source, source, s, 0, other).wait_send()

    sections = (mirror_ref, reflect_ref, through_ref, back_ref)
    middle_a = index_of(middle, y, z, 0)

    def rows(block, half):
        return W.at[block, pl.ds(half * (M // 2), M // 2)]

    def piece(part, half):
        return sections[part].at[0, pl.ds(half * (M // 2), M // 2)]

    def slot(block, half):
        return 2 * block + half

    def first_send(part, half):
        message(
            piece(part, half), rows(4 * x_half + part, half), 2 * part + half,
            slot(4 * x_half + part, half), middle_a,
        ).start()

    def turned(third):
        return (3, 2) if third else (2, 3)

    def later_send(order, half):
        @pl.when(y == 0)
        def _():
            first_send(turned(order == 2)[0], half)

        @pl.when(y > 0)
        def _():
            first_send(order, half)

    def pass_on(part, half, who):
        @pl.when(who)
        def _():
            got(rows(FQ + part, half), slot(FQ + part, half))
            got(rows(LQ + part, half), slot(LQ + part, half))

        at = 8 + 2 * part + half
        post(who & ((y == 1) | (y == 2)), rows(FQ + part, half), rows(LQ + part, half), at,
             slot(LQ + part, half), col(2 * (y - 1), 1))
        post(who & (y < 2), rows(LQ + part, half), rows(FQ + part, half), at + 8,
             slot(FQ + part, half), col(2 * y, 1))
        post(who & (y == 2), rows(LQ + part, half), rows(DQ + part, half), at + 8,
             slot(8 + part, half), col(2, 1))
        if part in (0, 3):
            first = 0 if part == 0 else 1
            post(who & (y == 0), rows(FQ + part, half), rows(HQ + first, half), at,
                 slot(14 + first, half), col(0, 1))
        else:
            post(who & (y == 3), rows(FQ + part, half), rows(R6 + part - 1, half), at,
                 slot(12 + part - 1, half), col(2, 1))

    def both_halves(block, receive):
        for half in (0, 1):
            got(rows(block, half), slot(receive, half))

    for part in (0, 1):
        for half in (0, 1):
            first_send(part, half)

    @pl.when(is_first_home)
    def _():
        pltpu.make_async_copy(through_ref.at[0], W.at[T3], local.at[1]).wait()
        pltpu.make_async_copy(reflect_ref.at[0], W.at[P3], local.at[2]).wait()
        V[TL] = mm(W[T3], incident_ref[...])
        V[RL] = mm(W[P3], incident_ref[...])

    post(is_first_home, V.at[TL], V.at[HT], 40, 36, index_of(middle, 0, z, 1))
    post(is_first_home, V.at[RL], V.at[HR], 41, 37, index_of(middle, 0, z, 1))
    post(is_first_home, V.at[TL], V.at[ENT], 42, 45, other)

    maps_copy.wait()
    for j in range(DEPTHS):
        maps_left[j * M : (j + 1) * M, :] = left(maps[j])

    for part in (0, 1):
        for half in (0, 1):
            pass_on(part, half, is_a)
            sent(piece(part, half), 2 * part + half)
            later_send(part + 2, half)

    @pl.when(is_mid)
    def _():
        @pl.when(c == 1)
        def _():
            for part in (0, 1):
                both_halves(FQ + part, FQ + part)
                both_halves(LQ + part, LQ + part)

        bounce, both = spread(W[FQ], W[LR])
        W[TX] = bounce
        W[TM] = both

    for half in (0, 1):
        pass_on(2, half, is_a & (y > 0))
        pass_on(3, half, is_a0)

    @pl.when(is_a0)
    def _():
        partial_value, full_value = summed(W[TX], W[TM], mm(W[FQ], W[LU]))
        W[TRP] = full_value
        W[CU] = mm(W[FU], W[LU] + mm(W[LR], partial_value))

    post(is_a0, W.at[CU], W.at[HU], 27, 35, col(1, 0))

    @pl.when(is_mid & ~is_a0)
    def _():
        @pl.when(c == 1)
        def _():
            both_halves(FT, FT)
            both_halves(LT, LT)

        g_through = summed(W[TX], W[TM], W[FT])[1]
        W[CT] = mm(W[LT], g_through)
        W[TRP] = mm(W[LR], g_through)

    for half in (0, 1):
        pass_on(3, half, is_a & (y > 0))
        pass_on(2, half, is_a0)

    @pl.when(is_a0)
    def _():
        W[CQ] = W[LQ] + mm(W[LT], W[TRP])

    post(is_a0, W.at[CQ], W.at[HQ], 26, 34, col(1, 0))

    @pl.when(is_a0)
    def _():
        value = summed(W[TX], W[TM], mm(W[FT], incident_ref[...]))[1]
        V[T01] = mm(W[LT], value)
        V[R01] = mm(W[FR], incident_ref[...]) + mm(W[FU], mm(W[LR], value))

    @pl.when(is_b2)
    def _():
        for part in range(4):
            both_halves(DQ + part, 8 + part)
        both_halves(R6, 12)
        both_halves(T6, 13)
        W[RIN], W[P3] = forward((W[DQ], W[DR], W[DT], W[DU]), W[R6])

    @pl.when(is_mid & ~is_a0)
    def _():
        @pl.when(c == 1)
        def _():
            both_halves(FU, FU)
            both_halves(LU, LU)

        W[CR] = W[FR] + mm(W[FU], W[TRP])

    post((is_a & (y >= 2)) | is_b2, W.at[CR], W.at[RIN], 24, 38,
         jnp.where(is_a, col(y - 1, 0), col(0, 1)))

    @pl.when(is_mid & ~is_a0)
    def _():
        partial_value, full_value = summed(W[TX], W[TM], mm(W[FQ], W[LU]))
        W[CQ] = W[LQ] + mm(W[LT], full_value)
        W[CU] = mm(W[FU], W[LU] + mm(W[LR], partial_value))

    post(is_a0, V.at[T01], V.at[HT], 28, 36, col(1, 0))
    post(is_a0, V.at[R01], V.at[HR], 29, 37, col(1, 0))
    post(is_a0, V.at[pl.ds(T01, 2)], V.at[pl.ds(TL, 2)], 30, 43, home(0, 1))
    post(is_a0, V.at[T01], V.at[ENT], 31, 45, 32 + residue + 1)

    def turn(step, carry):
        @pl.when((is_hub | is_two) & (step == 2 * c))
        def _():
            @pl.when(~is_b2)
            def _():
                got(W.at[RIN], 38)

            W[ROUT], W[POUT] = forward((W[CQ], W[CR], W[CT], W[CU]), W[RIN])

            @pl.when(is_two)
            def _():
                for half in (0, 1):
                    message(rows(ROUT, half), rows(R23, half), 25 + 18 * half, 39 + 8 * half,
                            col(1 + 2 * c, c)).start()

            @pl.when(is_a2)
            def _():
                message(W.at[POUT], W.at[POUT], 32, 40, col(3, 0)).start()

        @pl.when(is_hub & (step == 1))
        def _():
            got(V.at[HT], 36)
            got(V.at[HR], 37)

            @pl.when(is_a)
            def _():
                got(W.at[HQ], 34)
                got(W.at[HU], 35)

            @pl.when(c == 1)
            def _():
                both_halves(HQ, 14)
                both_halves(HU, 15)

            V[T01], V[R01], W[Q01], W[U01] = joined(
                W[HQ], W[HU], V[HT], V[HR], (W[CQ], W[CR], W[CT], W[CU])
            )

            @pl.when(is_a)
            def _():
                message(V.at[pl.ds(T01, 2)], V.at[pl.ds(TL, 2)], 30, 43, home(1, 1)).start()
                message(V.at[T01], V.at[ENT], 31, 45, 32 * 3 + residue + 1).start()

            @pl.when(c == 1)
            def _():
                message(V.at[pl.ds(T01, 2)], V.at[pl.ds(T01, 2)], 30, 46, col(1, 1)).start()

        return carry

    lax.fori_loop(0, 3, turn, 0)
    finals.append((is_two, rows(ROUT, 0), 25))
    finals.append((is_two, rows(ROUT, 1), 43))
    finals.append((is_a2, W.at[POUT], 32))
    finals.append((is_hub, V.at[pl.ds(T01, 2)], 30))
    finals.append((is_a1, V.at[T01], 31))

    for half in (0, 1):
        @pl.when(is_b3)
        def _():
            got(rows(R23, half), 39 + 8 * half)

        post(is_b3, rows(R23, half), rows(R23, half), 25 + 18 * half, 39 + 8 * half, col(0, 1))

    @pl.when(is_b1)
    def _():
        got(V.at[pl.ds(T01, 2)], 46)

    post(is_b1, V.at[pl.ds(T01, 2)], V.at[pl.ds(TL, 2)], 30, 43, home(1, 0))
    post(is_b1, V.at[T01], V.at[ENT], 31, 45, 32 * 2 + residue + 1)

    @pl.when(is_hub)
    def _():
        bounce = mm(W[HQ], W[ROUT])
        V[G2] = bounced(bounce, V[HT])
        V[P1] = mm(W[POUT], V[G2])

    post(is_hub, V.at[P1], V.at[PL], 34, 41, col(2, c))

    @pl.when(is_hub)
    def _():
        V[RB] = V[HR] + mm(W[HU], mm(W[ROUT], V[G2]))

    post(is_hub, V.at[RB], V.at[RL], 36, 44, home(2, chain_half))

    @pl.when(is_last)
    def _():
        @pl.when(is_a3)
        def _():
            got(W.at[POUT], 40)
            W[T3] = mm(W[CT], W[POUT])

        @pl.when(is_b2)
        def _():
            W[T3] = mm(W[T6], mm(W[P3], W[POUT]))

    @pl.when(is_hub)
    def _():
        got(rows(R23, 0), 39)
        got(rows(R23, 1), 47)
        bounce = mm(W[Q01], W[R23])
        V[G3] = bounced(bounce, V[T01])

    post(is_hub, V.at[G3], V.at[GL], 33, 42, jnp.where(is_a, col(3, 0), col(2, 1)))

    @pl.when(is_hub)
    def _():
        V[RC] = V[R01] + mm(W[U01], mm(W[R23], V[G3]))

    post(is_hub, V.at[RC], V.at[RL], 35, 44, home(3, chain_half))

    @pl.when(is_two)
    def _():
        got(V.at[PL], 41)
        V[TA] = mm(W[CT], V[PL])

    post(is_two, V.at[TA], V.at[ENT], 31, 45, 32 * (4 + chain_half) + residue + 1)
    post(is_two, V.at[TA], V.at[TL], 30, 43, home(2, chain_half))

    @pl.when(is_last)
    def _():
        got(V.at[GL], 42)
        V[TB] = mm(W[T3], V[GL])

    post(is_last & goes_on, V.at[TB], V.at[ENT], 38, 45, 32 * (6 + chain_half) + residue + 1)
    post(is_last, V.at[TB], V.at[TL], 37, 43, home(3, chain_half))

    @pl.when((y < 2) & ~is_first_home)
    def _():
        got(V.at[pl.ds(TL, 2)], 43)

    @pl.when(y >= 2)
    def _():
        got(V.at[TL], 43)
        got(V.at[RL], 44)

    through_copy = pltpu.make_async_copy(V.at[TL], through_out.at[0], local.at[3])
    reflected_copy = pltpu.make_async_copy(V.at[RL], reflected_out.at[0], local.at[4])
    through_copy.start()
    reflected_copy.start()

    @pl.when(me >= 1)
    def _():
        got(V.at[ENT], 45)

    @pl.when(me == 0)
    def _():
        V[ENT] = incident_ref[...]

    depth[...] = jnp.dot(maps_left[...], right(V[ENT]), preferred_element_type=F32).reshape(
        DEPTHS, M, INC
    )
    depth_copy = pltpu.make_async_copy(depth, depth_out.at[0], local.at[5])
    depth_copy.start()

    for part in (2, 3):
        for half in (0, 1):
            sent(piece(part, half), 2 * part + half)
    for condition, source, s in finals:
        @pl.when(condition)
        def _(source=source, s=s):
            sent(source, s)

    through_copy.wait()
    reflected_copy.wait()
    depth_copy.wait()


def results_kernel(through_ref, reflected_ref, depth_ref, through_out, reflected_out, depth_out, local):
    copies = [
        pltpu.make_async_copy(through_ref, through_out, local.at[0]),
        pltpu.make_async_copy(reflected_ref, reflected_out, local.at[1]),
    ]
    for j in range(DEPTHS):
        copies.append(pltpu.make_async_copy(depth_ref.at[0, j], depth_out.at[0, j], local.at[2 + j]))
    for copy in copies:
        copy.start()
    for copy in copies:
        copy.wait()


def per_device(front_reflect, front_through, back_reflect, back_through, depth_maps, incident):
    anywhere = pl.BlockSpec(memory_space=pl.ANY)
    results = (
        jax.ShapeDtypeStruct((1, M, INC), F32),
        jax.ShapeDtypeStruct((1, M, INC), F32),
        jax.ShapeDtypeStruct((1, DEPTHS, M, INC), F32),
    )
    made = pl.pallas_call(
        kernel,
        out_shape=results,
        in_specs=[anywhere] * 5 + [pl.BlockSpec(memory_space=pltpu.VMEM)],
        out_specs=(anywhere,) * 3,
        scratch_shapes=[
            pltpu.VMEM((BLOCKS, M, M), F32),
            pltpu.VMEM((VECS, M, INC), F32),
            pltpu.VMEM((DEPTHS, M, M), F32),
            pltpu.VMEM((DEPTHS * M, 3 * M), BF16),
            pltpu.VMEM((DEPTHS, M, INC), F32),
            pltpu.SemaphoreType.DMA((44,)),
            pltpu.SemaphoreType.DMA((48,)),
            pltpu.SemaphoreType.DMA((6,)),
        ],
        compiler_params=pltpu.CompilerParams(
            collective_id=0, has_side_effects=True, vmem_limit_bytes=60 * 2**20
        ),
        name="chains",
    )(front_reflect, front_through, back_reflect, back_through, depth_maps, incident)
    return pl.pallas_call(
        results_kernel,
        out_shape=results,
        in_specs=[anywhere] * 3,
        out_specs=(anywhere,) * 3,
        scratch_shapes=[pltpu.SemaphoreType.DMA((2 + DEPTHS,))],
        compiler_params=pltpu.CompilerParams(vmem_limit_bytes=60 * 2**20),
        name="results",
    )(*made)


def solution(mesh):
    in_specs = (
        P("sec", None, None),
        P("sec", None, None),
        P("sec", None, None),
        P("sec", None, None),
        P("sec", None, None, None),
        P(),
    )
    out_specs = (P("sec", None, None), P("sec", None, None), P("sec", None, None, None))
    return jax.shard_map(
        per_device, mesh=mesh, in_specs=in_specs, out_specs=out_specs, check_vma=False
    )
```

```python
import functools

import jax
import jax.numpy as jnp
from jax import lax
from jax.experimental import pallas as pl
from jax.experimental.pallas import tpu as pltpu
from jax.sharding import PartitionSpec as P


F32, BF16 = jnp.float32, jnp.bfloat16
MESH = pl.DeviceIdType.MESH
M, INC, DEPTHS = 384, 128, 4

FQ, FR, FT, FU, LQ, LR, LT, LU = range(8)
CQ, CR, CT, CU = range(8, 12)
DQ, DR, DT, DU, R6, T6 = range(12, 18)
HQ, HU, RIN, ROUT, POUT, R23, Q01, U01, T3, P3, TX, TM, TRP = range(18, 31)
BLOCKS = 31
HT, HR, T01, R01, G2, G3, P1, RB, RC, TA, TB, PL, GL, TL, RL, ENT = range(16)
VECS = 16


def halves(x):
    high = x.astype(BF16)
    return high, (x - high.astype(F32)).astype(BF16)


def left(x):
    high, low = halves(x)
    return jnp.concatenate([high, low, high], axis=1)


def right(x):
    high, low = halves(x)
    return jnp.concatenate([high, high, low], axis=0)


def mm(a, b):
    return jnp.dot(left(a), right(b), preferred_element_type=F32)


def spread(mirror, reflect):
    bounce = mm(mirror, reflect)
    return bounce, bounce + mm(bounce, bounce)


def summed(bounce, both, value):
    partial_value = value + mm(both, value)
    return partial_value, value + mm(bounce, partial_value)


def forward(former, latter_reflect):
    mirror, reflect, through, back = former
    bounce, both = spread(mirror, latter_reflect)
    g_through = summed(bounce, both, through)[1]
    return reflect + mm(back, mm(latter_reflect, g_through)), g_through


def bounced(bounce, field):
    value = field
    for _ in range(3):
        value = field + mm(bounce, value)
    return value


def joined(mirror, back, field, reflected, latter):
    own_mirror, own_reflect, own_through, own_back = latter
    cut = field.shape[1]
    bounce, both = spread(mirror, own_reflect)
    value = jnp.concatenate([field, mm(mirror, own_back)], axis=1)
    partial_value, full_value = summed(bounce, both, value)
    through = mm(own_through, full_value)
    turned = mm(own_reflect, jnp.concatenate([full_value[:, :cut], partial_value[:, cut:]], axis=1))
    returned = mm(back, jnp.concatenate([turned[:, :cut], own_back + turned[:, cut:]], axis=1))
    return (
        through[:, :cut],
        reflected + returned[:, :cut],
        own_mirror + through[:, cut:],
        returned[:, cut:],
    )


def index_of(x, y, z, c):
    return ((y * 4 + x) * 8 + z) * 2 + c


def middle_x(x, c):
    return lax.rem(x + jnp.where(x // 2 == c, 1, 3), 4)


def producer(k_half, y, middle, z):
    at = jnp.where(y == 3, 2 + k_half, y)
    return index_of(middle, at, z, 1 - k_half)


def kernel(
    reflect_ref, through_ref, mirror_ref, back_ref, maps_ref, incident_ref,
    through_out, reflected_out, depth_out,
    W, V, maps, maps_left, depth, send, recv, local,
):
    me = lax.axis_index("sec")
    c, z, x, y = me % 2, (me // 2) % 8, (me // 16) % 4, me // 64
    x_half = x // 2
    middle = middle_x(x, c)
    base = 1 - x % 2
    group_c = jnp.where(x % 2 == 1, x_half, 1 - x_half)
    residue = base * 16 + z * 2 + group_c
    chain_half = 1 - c

    def col(at_y, at_c):
        return index_of(x, at_y, z, at_c)

    def home(at_y, half):
        return index_of(base + 2 * half, at_y, z, group_c)

    is_a = c == 0
    is_mid = is_a | (y == 0) | (y == 2)
    is_hub = (is_a & (y == 1)) | ((c == 1) & (y == 0))
    is_two = y == 2
    is_a0, is_a2, is_a3 = is_a & (y == 0), is_a & (y == 2), is_a & (y == 3)
    is_b0, is_b2 = (c == 1) & (y == 0), (c == 1) & (y == 2)
    is_a1, is_b1 = is_a & (y == 1), (c == 1) & (y == 1)
    is_b3 = (c == 1) & (y == 3)
    is_last = is_a3 | is_b2
    is_first_home = (x_half == 0) & (y == 0)

    barrier = pltpu.get_barrier_semaphore()

    def greet(condition, device):
        @pl.when(condition)
        def _():
            pl.semaphore_signal(barrier, inc=1, device_id=(device,), device_id_type=MESH)

    def count(condition, n=1):
        return jnp.where(condition, n, 0)

    greet(is_a, home(y, 0))
    greet(is_a, home(y, 1))
    expected = 1
    greet(is_b0 | is_b2, col(y // 2 + 1, 0))
    expected += count(is_a & ((y == 1) | (y == 2)))
    greet(is_b0 | is_b2, col(y // 2, 0))
    expected += count(is_a & (y < 2))
    greet(is_b0, home(0, 0))
    expected += count(is_first_home)
    greet(is_b2, col(3, 0))
    expected += count(is_a3)
    greet(y == 1, col(0, c))
    expected += count(is_a0)
    greet(is_a & ((y == 1) | (y == 2)), col(y + 1, 0))
    greet(is_b0, col(2, 1))
    expected += count((is_a & (y >= 2)) | is_b2)
    greet(is_b3, col(2, 1))
    expected += count(is_b2)
    greet(is_b0, col(3, 1))
    expected += count(is_b3)
    greet(is_two, col(1 - c, c))
    expected += count(is_hub)
    greet(is_a3, col(1, 0))
    expected += count(is_a1)
    greet(is_a3, col(2, 0))
    expected += count(is_a2)
    greet((y == 0) & (x_half == 1), index_of(middle, 0, z, 0))
    expected += count(is_a0)
    greet((y >= 2) | ((y == 1) & (x_half == 1)), index_of(middle, x_half, z, 1 - x_half))
    expected += count(is_hub, 3)
    greet((y == 1) & (x_half == 0), index_of(middle, 1, z, 1))
    expected += count(is_b1)
    greet(y >= 2, producer(x_half, y, middle, z))
    expected += count(is_two) + count(is_last)
    before = jnp.maximum(me - 1, 0)
    bc, bz, bx, by = before % 2, (before // 2) % 8, (before // 16) % 4, before // 64
    first_before = (by == 0) & (bx // 2 == 0)
    greet(
        me >= 1,
        jnp.where(first_before, before, producer(bx // 2, by, middle_x(bx, bc), bz)),
    )
    goes_on = ~(is_a3 & (residue == 31))
    expected += count(is_first_home) + count(is_a0) + count(y == 1) + count(is_two)
    expected += count(is_last & goes_on)

    @pl.when(is_first_home)
    def _():
        pltpu.make_async_copy(through_ref.at[0], W.at[T3], local.at[1]).start()
        pltpu.make_async_copy(reflect_ref.at[0], W.at[P3], local.at[2]).start()

    maps_copy = pltpu.make_async_copy(maps_ref.at[0], maps, local.at[0])
    maps_copy.start()
    pl.semaphore_wait(barrier, expected)

    other = lax.rem(me + 1, lax.axis_size("sec"))

    def message(source, target, s, r, device):
        return pltpu.make_async_remote_copy(
            src_ref=source, dst_ref=target, send_sem=send.at[s], recv_sem=recv.at[r],
            device_id=(device,), device_id_type=MESH,
        )

    finals = []

    def post(condition, source, target, s, r, device):
        @pl.when(condition)
        def _():
            message(source, target, s, r, device).start()

        finals.append((condition, source, s))

    def got(target, r):
        message(target, target, 0, r, other).wait_recv()

    def sent(source, s):
        message(source, source, s, 0, other).wait_send()

    sections = (mirror_ref, reflect_ref, through_ref, back_ref)
    middle_a = index_of(middle, y, z, 0)

    def rows(block, half):
        return W.at[block, pl.ds(half * (M // 2), M // 2)]

    def piece(part, half):
        return sections[part].at[0, pl.ds(half * (M // 2), M // 2)]

    def slot(block, half):
        return 2 * block + half

    def first_send(part, half):
        message(
            piece(part, half), rows(4 * x_half + part, half), 2 * part + half,
            slot(4 * x_half + part, half), middle_a,
        ).start()

    def turned(third):
        return (3, 2) if third else (2, 3)

    def later_send(order, half):
        @pl.when(y == 0)
        def _():
            first_send(turned(order == 2)[0], half)

        @pl.when(y > 0)
        def _():
            first_send(order, half)

    def pass_on(part, half, who):
        @pl.when(who)
        def _():
            got(rows(FQ + part, half), slot(FQ + part, half))
            got(rows(LQ + part, half), slot(LQ + part, half))

        at = 8 + 2 * part + half
        post(who & ((y == 1) | (y == 2)), rows(FQ + part, half), rows(LQ + part, half), at,
             slot(LQ + part, half), col(2 * (y - 1), 1))
        post(who & (y < 2), rows(LQ + part, half), rows(FQ + part, half), at + 8,
             slot(FQ + part, half), col(2 * y, 1))
        post(who & (y == 2), rows(LQ + part, half), rows(DQ + part, half), at + 8,
             slot(8 + part, half), col(2, 1))
        if part in (0, 3):
            first = 0 if part == 0 else 1
            post(who & (y == 0), rows(FQ + part, half), rows(HQ + first, half), at,
                 slot(14 + first, half), col(0, 1))
        else:
            post(who & (y == 3), rows(FQ + part, half), rows(R6 + part - 1, half), at,
                 slot(12 + part - 1, half), col(2, 1))

    def both_halves(block, receive):
        for half in (0, 1):
            got(rows(block, half), slot(receive, half))

    for part in (0, 1):
        for half in (0, 1):
            first_send(part, half)

    @pl.when(is_first_home)
    def _():
        pltpu.make_async_copy(through_ref.at[0], W.at[T3], local.at[1]).wait()
        pltpu.make_async_copy(reflect_ref.at[0], W.at[P3], local.at[2]).wait()
        V[TL] = mm(W[T3], incident_ref[...])
        V[RL] = mm(W[P3], incident_ref[...])

    post(is_first_home, V.at[TL], V.at[HT], 40, 36, index_of(middle, 0, z, 1))
    post(is_first_home, V.at[RL], V.at[HR], 41, 37, index_of(middle, 0, z, 1))
    post(is_first_home, V.at[TL], V.at[ENT], 42, 45, other)

    maps_copy.wait()
    for j in range(DEPTHS):
        maps_left[j * M : (j + 1) * M, :] = left(maps[j])

    for part in (0, 1):
        for half in (0, 1):
            pass_on(part, half, is_a)
            sent(piece(part, half), 2 * part + half)
            later_send(part + 2, half)

    @pl.when(is_mid)
    def _():
        @pl.when(c == 1)
        def _():
            for part in (0, 1):
                both_halves(FQ + part, FQ + part)
                both_halves(LQ + part, LQ + part)

        bounce, both = spread(W[FQ], W[LR])
        W[TX] = bounce
        W[TM] = both

    for half in (0, 1):
        pass_on(2, half, is_a & (y > 0))
        pass_on(3, half, is_a0)

    @pl.when(is_a0)
    def _():
        partial_value, full_value = summed(W[TX], W[TM], mm(W[FQ], W[LU]))
        W[TRP] = full_value
        W[CU] = mm(W[FU], W[LU] + mm(W[LR], partial_value))

    post(is_a0, W.at[CU], W.at[HU], 27, 35, col(1, 0))

    @pl.when(is_mid & ~is_a0)
    def _():
        @pl.when(c == 1)
        def _():
            both_halves(FT, FT)
            both_halves(LT, LT)

        g_through = summed(W[TX], W[TM], W[FT])[1]
        W[CT] = mm(W[LT], g_through)
        W[TRP] = mm(W[LR], g_through)

    @pl.when(is_b2)
    def _():
        for part in (0, 1, 2):
            both_halves(DQ + part, 8 + part)
        both_halves(R6, 12)
        bounce, both = spread(W[DQ], W[R6])
        W[P3] = summed(bounce, both, W[DT])[1]
        W[T3] = mm(W[R6], W[P3])

    for half in (0, 1):
        pass_on(3, half, is_a & (y > 0))

        @pl.when(is_mid & ~is_a0)
        def _(half=half):
            here = pl.ds(half * (M // 2), M // 2)

            @pl.when(c == 1)
            def _():
                got(rows(FU, half), slot(FU, half))
                got(rows(LU, half), slot(LU, half))

            W[CR, here] = W[FR, here] + mm(W[FU, here], W[TRP])

        post((is_a & (y >= 2)) | is_b2, rows(CR, half), rows(RIN, half), 24 + 20 * half, 38 + 10 * half,
             jnp.where(is_a, col(y - 1, 0), col(0, 1)))

    for half in (0, 1):
        pass_on(2, half, is_a0)

    @pl.when(is_a0)
    def _():
        W[CQ] = W[LQ] + mm(W[LT], W[TRP])

    post(is_a0, W.at[CQ], W.at[HQ], 26, 34, col(1, 0))

    @pl.when(is_a0)
    def _():
        value = summed(W[TX], W[TM], mm(W[FT], incident_ref[...]))[1]
        V[T01] = mm(W[LT], value)
        V[R01] = mm(W[FR], incident_ref[...]) + mm(W[FU], mm(W[LR], value))

    @pl.when(is_b2)
    def _():
        both_halves(DU, 11)
        W[RIN] = W[DR] + mm(W[DU], W[T3])

    @pl.when(is_mid & ~is_a0)
    def _():
        partial_value, full_value = summed(W[TX], W[TM], mm(W[FQ], W[LU]))
        W[CQ] = W[LQ] + mm(W[LT], full_value)
        W[CU] = mm(W[FU], W[LU] + mm(W[LR], partial_value))

    post(is_a0, V.at[T01], V.at[HT], 28, 36, col(1, 0))
    post(is_a0, V.at[R01], V.at[HR], 29, 37, col(1, 0))
    post(is_a0, V.at[pl.ds(T01, 2)], V.at[pl.ds(TL, 2)], 30, 43, home(0, 1))
    post(is_a0, V.at[T01], V.at[ENT], 31, 45, 32 + residue + 1)

    def turn(step, carry):
        @pl.when((is_hub | is_two) & (step == 2 * c))
        def _():
            @pl.when(~is_b2)
            def _():
                got(rows(RIN, 0), 38)
                got(rows(RIN, 1), 48)

            W[ROUT], W[POUT] = forward((W[CQ], W[CR], W[CT], W[CU]), W[RIN])

            @pl.when(is_two)
            def _():
                for half in (0, 1):
                    message(rows(ROUT, half), rows(R23, half), 25 + 18 * half, 39 + 8 * half,
                            col(1 + 2 * c, c)).start()

            @pl.when(is_a2)
            def _():
                message(W.at[POUT], W.at[POUT], 32, 40, col(3, 0)).start()

        @pl.when(is_hub & (step == 1))
        def _():
            got(V.at[HT], 36)
            got(V.at[HR], 37)

            @pl.when(is_a)
            def _():
                got(W.at[HQ], 34)
                got(W.at[HU], 35)

            @pl.when(c == 1)
            def _():
                both_halves(HQ, 14)
                both_halves(HU, 15)

            V[T01], V[R01], W[Q01], W[U01] = joined(
                W[HQ], W[HU], V[HT], V[HR], (W[CQ], W[CR], W[CT], W[CU])
            )

            @pl.when(is_a)
            def _():
                message(V.at[pl.ds(T01, 2)], V.at[pl.ds(TL, 2)], 30, 43, home(1, 1)).start()
                message(V.at[T01], V.at[ENT], 31, 45, 32 * 3 + residue + 1).start()

            @pl.when(c == 1)
            def _():
                message(V.at[pl.ds(T01, 2)], V.at[pl.ds(T01, 2)], 30, 46, col(1, 1)).start()

        return carry

    lax.fori_loop(0, 3, turn, 0)
    finals.append((is_two, rows(ROUT, 0), 25))
    finals.append((is_two, rows(ROUT, 1), 43))
    finals.append((is_a2, W.at[POUT], 32))
    finals.append((is_hub, V.at[pl.ds(T01, 2)], 30))
    finals.append((is_a1, V.at[T01], 31))

    for half in (0, 1):
        @pl.when(is_b3)
        def _():
            got(rows(R23, half), 39 + 8 * half)

        post(is_b3, rows(R23, half), rows(R23, half), 25 + 18 * half, 39 + 8 * half, col(0, 1))

    @pl.when(is_b1)
    def _():
        got(V.at[pl.ds(T01, 2)], 46)

    post(is_b1, V.at[pl.ds(T01, 2)], V.at[pl.ds(TL, 2)], 30, 43, home(1, 0))
    post(is_b1, V.at[T01], V.at[ENT], 31, 45, 32 * 2 + residue + 1)

    @pl.when(is_hub)
    def _():
        bounce = mm(W[HQ], W[ROUT])
        V[G2] = bounced(bounce, V[HT])
        V[P1] = mm(W[POUT], V[G2])

    post(is_hub, V.at[P1], V.at[PL], 34, 41, col(2, c))

    @pl.when(is_hub)
    def _():
        V[RB] = V[HR] + mm(W[HU], mm(W[ROUT], V[G2]))

    post(is_hub, V.at[RB], V.at[RL], 36, 44, home(2, chain_half))

    @pl.when(is_last)
    def _():
        @pl.when(is_a3)
        def _():
            got(W.at[POUT], 40)
            W[T3] = mm(W[CT], W[POUT])

        @pl.when(is_b2)
        def _():
            both_halves(T6, 13)
            W[T3] = mm(W[T6], mm(W[P3], W[POUT]))

    @pl.when(is_hub)
    def _():
        got(rows(R23, 0), 39)
        got(rows(R23, 1), 47)
        bounce = mm(W[Q01], W[R23])
        V[G3] = bounced(bounce, V[T01])

    post(is_hub, V.at[G3], V.at[GL], 33, 42, jnp.where(is_a, col(3, 0), col(2, 1)))

    @pl.when(is_hub)
    def _():
        V[RC] = V[R01] + mm(W[U01], mm(W[R23], V[G3]))

    post(is_hub, V.at[RC], V.at[RL], 35, 44, home(3, chain_half))

    @pl.when(is_two)
    def _():
        got(V.at[PL], 41)
        V[TA] = mm(W[CT], V[PL])

    post(is_two, V.at[TA], V.at[ENT], 31, 45, 32 * (4 + chain_half) + residue + 1)
    post(is_two, V.at[TA], V.at[TL], 30, 43, home(2, chain_half))

    @pl.when(is_last)
    def _():
        got(V.at[GL], 42)
        V[TB] = mm(W[T3], V[GL])

    post(is_last & goes_on, V.at[TB], V.at[ENT], 38, 45, 32 * (6 + chain_half) + residue + 1)
    post(is_last, V.at[TB], V.at[TL], 37, 43, home(3, chain_half))

    @pl.when((y < 2) & ~is_first_home)
    def _():
        got(V.at[pl.ds(TL, 2)], 43)

    @pl.when(y >= 2)
    def _():
        got(V.at[TL], 43)
        got(V.at[RL], 44)

    through_copy = pltpu.make_async_copy(V.at[TL], through_out.at[0], local.at[3])
    reflected_copy = pltpu.make_async_copy(V.at[RL], reflected_out.at[0], local.at[4])
    through_copy.start()
    reflected_copy.start()

    @pl.when(me >= 1)
    def _():
        got(V.at[ENT], 45)

    @pl.when(me == 0)
    def _():
        V[ENT] = incident_ref[...]

    depth[...] = jnp.dot(maps_left[...], right(V[ENT]), preferred_element_type=F32).reshape(
        DEPTHS, M, INC
    )
    depth_copy = pltpu.make_async_copy(depth, depth_out.at[0], local.at[5])
    depth_copy.start()

    for part in (2, 3):
        for half in (0, 1):
            sent(piece(part, half), 2 * part + half)
    for condition, source, s in finals:
        @pl.when(condition)
        def _(source=source, s=s):
            sent(source, s)

    through_copy.wait()
    reflected_copy.wait()
    depth_copy.wait()


def results_kernel(through_ref, reflected_ref, depth_ref, through_out, reflected_out, depth_out):
    through_out[...] = through_ref[...]
    reflected_out[...] = reflected_ref[...]
    depth_out[...] = depth_ref[...]


def per_device(front_reflect, front_through, back_reflect, back_through, depth_maps, incident):
    anywhere = pl.BlockSpec(memory_space=pl.ANY)
    results = (
        jax.ShapeDtypeStruct((1, M, INC), F32),
        jax.ShapeDtypeStruct((1, M, INC), F32),
        jax.ShapeDtypeStruct((1, DEPTHS, M, INC), F32),
    )
    made = pl.pallas_call(
        kernel,
        out_shape=results,
        in_specs=[anywhere] * 5 + [pl.BlockSpec(memory_space=pltpu.VMEM)],
        out_specs=(anywhere,) * 3,
        scratch_shapes=[
            pltpu.VMEM((BLOCKS, M, M), F32),
            pltpu.VMEM((VECS, M, INC), F32),
            pltpu.VMEM((DEPTHS, M, M), F32),
            pltpu.VMEM((DEPTHS * M, 3 * M), BF16),
            pltpu.VMEM((DEPTHS, M, INC), F32),
            pltpu.SemaphoreType.DMA((45,)),
            pltpu.SemaphoreType.DMA((49,)),
            pltpu.SemaphoreType.DMA((6,)),
        ],
        compiler_params=pltpu.CompilerParams(
            collective_id=0, has_side_effects=True, vmem_limit_bytes=60 * 2**20
        ),
        name="chains",
    )(front_reflect, front_through, back_reflect, back_through, depth_maps, incident)
    return pl.pallas_call(
        results_kernel,
        out_shape=results,
        in_specs=[pl.BlockSpec(memory_space=pltpu.VMEM)] * 3,
        out_specs=(pl.BlockSpec(memory_space=pltpu.VMEM),) * 3,
        name="results",
    )(*made)


def solution(mesh):
    in_specs = (
        P("sec", None, None),
        P("sec", None, None),
        P("sec", None, None),
        P("sec", None, None),
        P("sec", None, None, None),
        P(),
    )
    out_specs = (P("sec", None, None), P("sec", None, None), P("sec", None, None, None))
    return jax.shard_map(
        per_device, mesh=mesh, in_specs=in_specs, out_specs=out_specs, check_vma=False
    )
```

```python
import functools

import jax
import jax.numpy as jnp
from jax import lax
from jax.experimental import pallas as pl
from jax.experimental.pallas import tpu as pltpu
from jax.sharding import PartitionSpec as P


F32, BF16 = jnp.float32, jnp.bfloat16
MESH = pl.DeviceIdType.MESH
M, INC, DEPTHS = 384, 128, 4

FQ, FR, FT, FU, LQ, LR, LT, LU = range(8)
CQ, CR, CT, CU = range(8, 12)
DQ, DR, DT, DU, R6, T6 = range(12, 18)
HQ, HU, RIN, ROUT, POUT, R23, Q01, U01, T3, P3, TX, TM, TRP = range(18, 31)
BLOCKS = 31
HT, HR, T01, R01, G2, G3, P1, RB, RC, TA, TB, PL, GL, TL, RL, ENT = range(16)
VECS = 16


def halves(x):
    high = x.astype(BF16)
    return high, (x - high.astype(F32)).astype(BF16)


def left(x):
    high, low = halves(x)
    return jnp.concatenate([high, low, high], axis=1)


def right(x):
    high, low = halves(x)
    return jnp.concatenate([high, high, low], axis=0)


def mm(a, b):
    return jnp.dot(left(a), right(b), preferred_element_type=F32)


def spread(mirror, reflect):
    bounce = mm(mirror, reflect)
    return bounce, bounce + mm(bounce, bounce)


def summed(bounce, both, value):
    partial_value = value + mm(both, value)
    return partial_value, value + mm(bounce, partial_value)


def bounced(bounce, field):
    value = field
    for _ in range(3):
        value = field + mm(bounce, value)
    return value


def index_of(x, y, z, c):
    return ((y * 4 + x) * 8 + z) * 2 + c


def middle_x(x, c):
    return lax.rem(x + jnp.where(x // 2 == c, 1, 3), 4)


def producer(k_half, y, middle, z):
    at = jnp.where(y == 3, 2 + k_half, y)
    return index_of(middle, at, z, 1 - k_half)


def kernel(
    reflect_ref, through_ref, mirror_ref, back_ref, maps_ref, incident_ref,
    through_out, reflected_out, depth_out,
    W, V, maps, maps_left, depth, send, recv, local,
):
    me = lax.axis_index("sec")
    c, z, x, y = me % 2, (me // 2) % 8, (me // 16) % 4, me // 64
    x_half = x // 2
    middle = middle_x(x, c)
    base = 1 - x % 2
    group_c = jnp.where(x % 2 == 1, x_half, 1 - x_half)
    residue = base * 16 + z * 2 + group_c
    chain_half = 1 - c

    def col(at_y, at_c):
        return index_of(x, at_y, z, at_c)

    def home(at_y, half):
        return index_of(base + 2 * half, at_y, z, group_c)

    is_a = c == 0
    is_mid = is_a | (y == 0) | (y == 2)
    is_hub = (is_a & (y == 1)) | ((c == 1) & (y == 0))
    is_two = y == 2
    is_a0, is_a2, is_a3 = is_a & (y == 0), is_a & (y == 2), is_a & (y == 3)
    is_b0, is_b2 = (c == 1) & (y == 0), (c == 1) & (y == 2)
    is_a1, is_b1 = is_a & (y == 1), (c == 1) & (y == 1)
    is_last = is_a3 | is_b2
    is_first_home = (x_half == 0) & (y == 0)

    barrier = pltpu.get_barrier_semaphore()

    def greet(condition, device):
        @pl.when(condition)
        def _():
            pl.semaphore_signal(barrier, inc=1, device_id=(device,), device_id_type=MESH)

    def count(condition, n=1):
        return jnp.where(condition, n, 0)

    greet(is_a, home(y, 0))
    greet(is_a, home(y, 1))
    expected = 1
    greet(is_b0 | is_b2, col(y // 2 + 1, 0))
    expected += count(is_a & ((y == 1) | (y == 2)))
    greet(is_b0 | is_b2, col(y // 2, 0))
    expected += count(is_a & (y < 2))
    greet(is_b0, home(0, 0))
    expected += count(is_first_home)
    greet(is_b2, col(3, 0))
    expected += count(is_a3)
    greet(y == 1, col(0, c))
    expected += count(is_a0)
    greet(is_a & ((y == 1) | (y == 2)), col(y + 1, 0))
    greet(is_b0, col(2, 1))
    expected += count((is_a & (y >= 2)) | is_b2)
    greet(is_two, col(1 - c, c))
    expected += count(is_hub)
    greet(is_a3, col(1, 0))
    expected += count(is_a1)
    greet(is_a3, col(2, 0))
    expected += count(is_a2)
    greet((y == 0) & (x_half == 1), index_of(middle, 0, z, 0))
    expected += count(is_a0)
    greet((y >= 2) | ((y == 1) & (x_half == 1)), index_of(middle, x_half, z, 1 - x_half))
    expected += count(is_hub, 3)
    greet((y == 1) & (x_half == 0), index_of(middle, 1, z, 1))
    expected += count(is_b1)
    greet(y >= 2, producer(x_half, y, middle, z))
    expected += count(is_two) + count(is_last)
    before = jnp.maximum(me - 1, 0)
    bc, bz, bx, by = before % 2, (before // 2) % 8, (before // 16) % 4, before // 64
    first_before = (by == 0) & (bx // 2 == 0)
    greet(
        me >= 1,
        jnp.where(first_before, before, producer(bx // 2, by, middle_x(bx, bc), bz)),
    )
    goes_on = ~(is_a3 & (residue == 31))
    expected += count(is_first_home) + count(is_a0) + count(y == 1) + count(is_two)
    expected += count(is_last & goes_on)

    @pl.when(is_first_home)
    def _():
        pltpu.make_async_copy(through_ref.at[0], W.at[T3], local.at[1]).start()
        pltpu.make_async_copy(reflect_ref.at[0], W.at[P3], local.at[2]).start()

    maps_copy = pltpu.make_async_copy(maps_ref.at[0], maps, local.at[0])
    maps_copy.start()
    pl.semaphore_wait(barrier, expected)

    other = lax.rem(me + 1, lax.axis_size("sec"))

    def message(source, target, s, r, device):
        return pltpu.make_async_remote_copy(
            src_ref=source, dst_ref=target, send_sem=send.at[s], recv_sem=recv.at[r],
            device_id=(device,), device_id_type=MESH,
        )

    finals = []

    def post(condition, source, target, s, r, device):
        @pl.when(condition)
        def _():
            message(source, target, s, r, device).start()

        finals.append((condition, source, s))

    def got(target, r):
        message(target, target, 0, r, other).wait_recv()

    def sent(source, s):
        message(source, source, s, 0, other).wait_send()

    sections = (mirror_ref, reflect_ref, through_ref, back_ref)
    middle_a = index_of(middle, y, z, 0)

    def rows(block, half):
        return W.at[block, pl.ds(half * (M // 2), M // 2)]

    def piece(part, half):
        return sections[part].at[0, pl.ds(half * (M // 2), M // 2)]

    def slot(block, half):
        return 2 * block + half

    def first_send(part, half):
        message(
            piece(part, half), rows(4 * x_half + part, half), 2 * part + half,
            slot(4 * x_half + part, half), middle_a,
        ).start()

    def turned(third):
        return (3, 2) if third else (2, 3)

    def later_send(order, half):
        @pl.when(y == 0)
        def _():
            first_send(turned(order == 2)[0], half)

        @pl.when(y > 0)
        def _():
            first_send(order, half)

    def pass_on(part, half, who):
        @pl.when(who)
        def _():
            got(rows(FQ + part, half), slot(FQ + part, half))
            got(rows(LQ + part, half), slot(LQ + part, half))

        at = 8 + 2 * part + half
        post(who & ((y == 1) | (y == 2)), rows(FQ + part, half), rows(LQ + part, half), at,
             slot(LQ + part, half), col(2 * (y - 1), 1))
        post(who & (y < 2), rows(LQ + part, half), rows(FQ + part, half), at + 8,
             slot(FQ + part, half), col(2 * y, 1))
        post(who & (y == 2), rows(LQ + part, half), rows(DQ + part, half), at + 8,
             slot(8 + part, half), col(2, 1))
        if part in (0, 3):
            first = 0 if part == 0 else 1
            post(who & (y == 0), rows(FQ + part, half), rows(HQ + first, half), at,
                 slot(14 + first, half), col(0, 1))
        else:
            post(who & (y == 3), rows(FQ + part, half), rows(R6 + part - 1, half), at,
                 slot(12 + part - 1, half), col(2, 1))

    def both_halves(block, receive):
        for half in (0, 1):
            got(rows(block, half), slot(receive, half))

    for part in (0, 1):
        for half in (0, 1):
            first_send(part, half)

    @pl.when(is_first_home)
    def _():
        pltpu.make_async_copy(through_ref.at[0], W.at[T3], local.at[1]).wait()
        pltpu.make_async_copy(reflect_ref.at[0], W.at[P3], local.at[2]).wait()
        V[TL] = mm(W[T3], incident_ref[...])
        V[RL] = mm(W[P3], incident_ref[...])

    post(is_first_home, V.at[TL], V.at[HT], 40, 36, index_of(middle, 0, z, 1))
    post(is_first_home, V.at[RL], V.at[HR], 41, 37, index_of(middle, 0, z, 1))
    post(is_first_home, V.at[TL], V.at[ENT], 42, 45, other)

    maps_copy.wait()
    for j in range(DEPTHS):
        maps_left[j * M : (j + 1) * M, :] = left(maps[j])

    for part in (0, 1):
        for half in (0, 1):
            pass_on(part, half, is_a)
            sent(piece(part, half), 2 * part + half)
            later_send(part + 2, half)

    @pl.when(is_mid)
    def _():
        @pl.when(c == 1)
        def _():
            for part in (0, 1):
                both_halves(FQ + part, FQ + part)
                both_halves(LQ + part, LQ + part)

        bounce, both = spread(W[FQ], W[LR])
        W[TX] = bounce
        W[TM] = both

    for half in (0, 1):
        pass_on(2, half, is_a & (y > 0))
        pass_on(3, half, is_a0)

    @pl.when(is_a0)
    def _():
        partial_value, full_value = summed(W[TX], W[TM], mm(W[FQ], W[LU]))
        W[TRP] = full_value
        W[CU] = mm(W[FU], W[LU] + mm(W[LR], partial_value))

    post(is_a0, W.at[CU], W.at[HU], 27, 35, col(1, 0))

    @pl.when(is_mid & ~is_a0)
    def _():
        @pl.when(c == 1)
        def _():
            both_halves(FT, FT)
            both_halves(LT, LT)

        g_through = summed(W[TX], W[TM], W[FT])[1]
        W[CT] = mm(W[LT], g_through)
        W[TRP] = mm(W[LR], g_through)

    @pl.when(is_b2)
    def _():
        for part in (0, 1, 2):
            both_halves(DQ + part, 8 + part)
        both_halves(R6, 12)
        bounce, both = spread(W[DQ], W[R6])
        W[P3] = summed(bounce, both, W[DT])[1]
        W[T3] = mm(W[R6], W[P3])
        both_halves(DU, 11)
        W[RIN] = W[DR] + mm(W[DU], W[T3])

    for half in (0, 1):
        pass_on(3, half, is_a & (y > 0))

        @pl.when(is_mid & ~is_a0)
        def _(half=half):
            here = pl.ds(half * (M // 2), M // 2)

            @pl.when(c == 1)
            def _():
                got(rows(FU, half), slot(FU, half))
                got(rows(LU, half), slot(LU, half))

            W[CR, here] = W[FR, here] + mm(W[FU, here], W[TRP])

        post((is_a & (y >= 2)) | is_b2, rows(CR, half), rows(RIN, half), 24 + 20 * half, 38 + 10 * half,
             jnp.where(is_a, col(y - 1, 0), col(0, 1)))

    for half in (0, 1):
        pass_on(2, half, is_a0)

    @pl.when(is_a0)
    def _():
        W[CQ] = W[LQ] + mm(W[LT], W[TRP])

    post(is_a0, W.at[CQ], W.at[HQ], 26, 34, col(1, 0))

    @pl.when(is_a0)
    def _():
        value = summed(W[TX], W[TM], mm(W[FT], incident_ref[...]))[1]
        V[T01] = mm(W[LT], value)
        V[R01] = mm(W[FR], incident_ref[...]) + mm(W[FU], mm(W[LR], value))

    @pl.when(is_mid & ~is_a0)
    def _():
        partial_value, full_value = summed(W[TX], W[TM], mm(W[FQ], W[LU]))
        W[CQ] = W[LQ] + mm(W[LT], full_value)
        W[CU] = mm(W[FU], W[LU] + mm(W[LR], partial_value))

    post(is_a0, V.at[T01], V.at[HT], 28, 36, col(1, 0))
    post(is_a0, V.at[R01], V.at[HR], 29, 37, col(1, 0))
    post(is_a0, V.at[pl.ds(T01, 2)], V.at[pl.ds(TL, 2)], 30, 43, home(0, 1))
    post(is_a0, V.at[T01], V.at[ENT], 31, 45, 32 + residue + 1)

    def turn(step, carry):
        @pl.when((is_hub | is_two) & (step == 2 * c))
        def _():
            @pl.when(~is_b2)
            def _():
                got(rows(RIN, 0), 38)
                got(rows(RIN, 1), 48)

            bounce, both = spread(W[CQ], W[RIN])
            W[POUT] = summed(bounce, both, W[CT])[1]
            W[TRP] = mm(W[RIN], W[POUT])
            for half in (0, 1):
                here = pl.ds(half * (M // 2), M // 2)
                W[ROUT, here] = W[CR, here] + mm(W[CU, here], W[TRP])

                @pl.when(is_two)
                def _(half=half):
                    message(rows(ROUT, half), rows(R23, half), 25 + 18 * half, 39 + 8 * half,
                            col(1 - c, c)).start()

            @pl.when(is_a2)
            def _():
                message(W.at[POUT], W.at[POUT], 32, 40, col(3, 0)).start()

        @pl.when(is_hub & (step == 1))
        def _():
            @pl.when(is_a)
            def _():
                got(W.at[HQ], 34)

            @pl.when(c == 1)
            def _():
                both_halves(HQ, 14)

            bounce, both = spread(W[HQ], W[CR])
            W[TX] = bounce
            W[TM] = both
            W[TRP] = mm(W[HQ], W[CU])
            got(V.at[HT], 36)
            value = jnp.concatenate([V[HT], W[TRP]], axis=1)
            partial_value, full_value = summed(W[TX], W[TM], value)
            through = mm(W[CT], full_value)
            V[T01] = through[:, :INC]
            W[Q01] = W[CQ] + through[:, INC:]
            back = mm(W[CR], jnp.concatenate([full_value[:, :INC], partial_value[:, INC:]], axis=1))
            V[G2] = back[:, :INC]
            W[TRP] = W[CU] + back[:, INC:]

            @pl.when(is_a)
            def _():
                got(W.at[HU], 35)

            @pl.when(c == 1)
            def _():
                both_halves(HU, 15)

            returned = mm(W[HU], jnp.concatenate([V[G2], W[TRP]], axis=1))
            W[U01] = returned[:, INC:]
            got(V.at[HR], 37)
            V[R01] = V[HR] + returned[:, :INC]

            @pl.when(is_a)
            def _():
                message(V.at[pl.ds(T01, 2)], V.at[pl.ds(TL, 2)], 30, 43, home(1, 1)).start()
                message(V.at[T01], V.at[ENT], 31, 45, 32 * 3 + residue + 1).start()

            @pl.when(c == 1)
            def _():
                message(V.at[pl.ds(T01, 2)], V.at[pl.ds(T01, 2)], 30, 46, col(1, 1)).start()

        return carry

    lax.fori_loop(0, 3, turn, 0)
    finals.append((is_two, rows(ROUT, 0), 25))
    finals.append((is_two, rows(ROUT, 1), 43))
    finals.append((is_a2, W.at[POUT], 32))
    finals.append((is_hub, V.at[pl.ds(T01, 2)], 30))
    finals.append((is_a1, V.at[T01], 31))

    @pl.when(is_b1)
    def _():
        got(V.at[pl.ds(T01, 2)], 46)

    post(is_b1, V.at[pl.ds(T01, 2)], V.at[pl.ds(TL, 2)], 30, 43, home(1, 0))
    post(is_b1, V.at[T01], V.at[ENT], 31, 45, 32 * 2 + residue + 1)

    def last_fields(step, carry):
        @pl.when(is_hub & (step == chain_half))
        def _():
            bounce = mm(W[HQ], W[ROUT])
            V[G2] = bounced(bounce, V[HT])
            V[P1] = mm(W[POUT], V[G2])
            message(V.at[P1], V.at[PL], 34, 41, col(2, c)).start()
            V[RB] = V[HR] + mm(W[HU], mm(W[ROUT], V[G2]))
            message(V.at[RB], V.at[RL], 36, 44, home(2, chain_half)).start()

        @pl.when(is_hub & (step == c))
        def _():
            got(rows(R23, 0), 39)
            got(rows(R23, 1), 47)
            bounce = mm(W[Q01], W[R23])
            V[G3] = bounced(bounce, V[T01])
            message(V.at[G3], V.at[GL], 33, 42, jnp.where(is_a, col(3, 0), col(2, 1))).start()
            V[RC] = V[R01] + mm(W[U01], mm(W[R23], V[G3]))
            message(V.at[RC], V.at[RL], 35, 44, home(3, chain_half)).start()

        return carry

    lax.fori_loop(0, 2, last_fields, 0)
    finals.append((is_hub, V.at[P1], 34))
    finals.append((is_hub, V.at[RB], 36))
    finals.append((is_hub, V.at[G3], 33))
    finals.append((is_hub, V.at[RC], 35))

    @pl.when(is_last)
    def _():
        @pl.when(is_a3)
        def _():
            got(W.at[POUT], 40)
            W[T3] = mm(W[CT], W[POUT])

        @pl.when(is_b2)
        def _():
            both_halves(T6, 13)
            W[T3] = mm(W[T6], mm(W[P3], W[POUT]))

    @pl.when(is_two)
    def _():
        got(V.at[PL], 41)
        V[TA] = mm(W[CT], V[PL])

    post(is_two, V.at[TA], V.at[ENT], 31, 45, 32 * (4 + chain_half) + residue + 1)
    post(is_two, V.at[TA], V.at[TL], 30, 43, home(2, chain_half))

    @pl.when(is_last)
    def _():
        got(V.at[GL], 42)
        V[TB] = mm(W[T3], V[GL])

    post(is_last & goes_on, V.at[TB], V.at[ENT], 38, 45, 32 * (6 + chain_half) + residue + 1)
    post(is_last, V.at[TB], V.at[TL], 37, 43, home(3, chain_half))

    @pl.when((y < 2) & ~is_first_home)
    def _():
        got(V.at[pl.ds(TL, 2)], 43)

    @pl.when(y >= 2)
    def _():
        got(V.at[TL], 43)
        got(V.at[RL], 44)

    through_copy = pltpu.make_async_copy(V.at[TL], through_out.at[0], local.at[3])
    reflected_copy = pltpu.make_async_copy(V.at[RL], reflected_out.at[0], local.at[4])
    through_copy.start()
    reflected_copy.start()

    @pl.when(me >= 1)
    def _():
        got(V.at[ENT], 45)

    @pl.when(me == 0)
    def _():
        V[ENT] = incident_ref[...]

    depth[...] = jnp.dot(maps_left[...], right(V[ENT]), preferred_element_type=F32).reshape(
        DEPTHS, M, INC
    )
    depth_copy = pltpu.make_async_copy(depth, depth_out.at[0], local.at[5])
    depth_copy.start()

    for part in (2, 3):
        for half in (0, 1):
            sent(piece(part, half), 2 * part + half)
    for condition, source, s in finals:
        @pl.when(condition)
        def _(source=source, s=s):
            sent(source, s)

    through_copy.wait()
    reflected_copy.wait()
    depth_copy.wait()


def results_kernel(through_ref, reflected_ref, depth_ref, through_out, reflected_out, depth_out):
    through_out[...] = through_ref[...]
    reflected_out[...] = reflected_ref[...]
    depth_out[...] = depth_ref[...]


def per_device(front_reflect, front_through, back_reflect, back_through, depth_maps, incident):
    anywhere = pl.BlockSpec(memory_space=pl.ANY)
    results = (
        jax.ShapeDtypeStruct((1, M, INC), F32),
        jax.ShapeDtypeStruct((1, M, INC), F32),
        jax.ShapeDtypeStruct((1, DEPTHS, M, INC), F32),
    )
    made = pl.pallas_call(
        kernel,
        out_shape=results,
        in_specs=[anywhere] * 5 + [pl.BlockSpec(memory_space=pltpu.VMEM)],
        out_specs=(anywhere,) * 3,
        scratch_shapes=[
            pltpu.VMEM((BLOCKS, M, M), F32),
            pltpu.VMEM((VECS, M, INC), F32),
            pltpu.VMEM((DEPTHS, M, M), F32),
            pltpu.VMEM((DEPTHS * M, 3 * M), BF16),
            pltpu.VMEM((DEPTHS, M, INC), F32),
            pltpu.SemaphoreType.DMA((45,)),
            pltpu.SemaphoreType.DMA((49,)),
            pltpu.SemaphoreType.DMA((6,)),
        ],
        compiler_params=pltpu.CompilerParams(
            collective_id=0, has_side_effects=True, vmem_limit_bytes=60 * 2**20
        ),
        name="chains",
    )(front_reflect, front_through, back_reflect, back_through, depth_maps, incident)
    return pl.pallas_call(
        results_kernel,
        out_shape=results,
        in_specs=[pl.BlockSpec(memory_space=pltpu.VMEM)] * 3,
        out_specs=(pl.BlockSpec(memory_space=pltpu.VMEM),) * 3,
        name="results",
    )(*made)


def solution(mesh):
    in_specs = (
        P("sec", None, None),
        P("sec", None, None),
        P("sec", None, None),
        P("sec", None, None),
        P("sec", None, None, None),
        P(),
    )
    out_specs = (P("sec", None, None), P("sec", None, None), P("sec", None, None, None))
    return jax.shard_map(
        per_device, mesh=mesh, in_specs=in_specs, out_specs=out_specs, check_vma=False
    )
```

```python
import functools

import jax
import jax.numpy as jnp
from jax import lax
from jax.experimental import pallas as pl
from jax.experimental.pallas import tpu as pltpu
from jax.sharding import PartitionSpec as P


F32, BF16 = jnp.float32, jnp.bfloat16
MESH = pl.DeviceIdType.MESH
M, INC, DEPTHS = 384, 128, 4

FQ, FR, FT, FU, LQ, LR, LT, LU = range(8)
CQ, CR, CT, CU = range(8, 12)
DQ, DR, DT, DU, R6, T6 = range(12, 18)
HQ, HU, RIN, ROUT, POUT, R23, Q01, U01, T3, P3, TX, TM, TRP = range(18, 31)
BLOCKS = 31
HT, HR, T01, R01, G2, G3, P1, RB, RC, TA, TB, PL, GL, TL, RL, ENT = range(16)
VECS = 16


def halves(x):
    high = x.astype(BF16)
    return high, (x - high.astype(F32)).astype(BF16)


def left(x):
    high, low = halves(x)
    return jnp.concatenate([high, low, high], axis=1)


def right(x):
    high, low = halves(x)
    return jnp.concatenate([high, high, low], axis=0)


def mm(a, b):
    return jnp.dot(left(a), right(b), preferred_element_type=F32)


def spread(mirror, reflect):
    bounce = mm(mirror, reflect)
    return bounce, bounce + mm(bounce, bounce)


def summed(bounce, both, value):
    partial_value = value + mm(both, value)
    return partial_value, value + mm(bounce, partial_value)


def bounced(bounce, field):
    value = field
    for _ in range(3):
        value = field + mm(bounce, value)
    return value


def index_of(x, y, z, c):
    return ((y * 4 + x) * 8 + z) * 2 + c


def middle_x(x, c):
    return lax.rem(x + jnp.where(x // 2 == c, 1, 3), 4)


def producer(k_half, y, middle, z):
    return index_of(middle, y, z, 1 - k_half)


def kernel(
    reflect_ref, through_ref, mirror_ref, back_ref, maps_ref, incident_ref,
    through_out, reflected_out, depth_out,
    W, V, maps, maps_left, depth, send, recv, local,
):
    me = lax.axis_index("sec")
    c, z, x, y = me % 2, (me // 2) % 8, (me // 16) % 4, me // 64
    x_half = x // 2
    middle = middle_x(x, c)
    base = 1 - x % 2
    group_c = jnp.where(x % 2 == 1, x_half, 1 - x_half)
    residue = base * 16 + z * 2 + group_c
    chain_half = 1 - c

    def col(at_y, at_c):
        return index_of(x, at_y, z, at_c)

    def home(at_y, half):
        return index_of(base + 2 * half, at_y, z, group_c)

    is_a = c == 0
    is_mid = is_a | (y == 0) | (y == 2)
    is_hub = (is_a & (y == 1)) | ((c == 1) & (y == 0))
    is_two = y == 2
    is_a0, is_a2, is_a3 = is_a & (y == 0), is_a & (y == 2), is_a & (y == 3)
    is_b0, is_b2 = (c == 1) & (y == 0), (c == 1) & (y == 2)
    is_a1, is_b1 = is_a & (y == 1), (c == 1) & (y == 1)
    is_last = y == 3
    is_first_home = (x_half == 0) & (y == 0)

    barrier = pltpu.get_barrier_semaphore()

    def greet(condition, device):
        @pl.when(condition)
        def _():
            pl.semaphore_signal(barrier, inc=1, device_id=(device,), device_id_type=MESH)

    def count(condition, n=1):
        return jnp.where(condition, n, 0)

    greet(is_a, home(y, 0))
    greet(is_a, home(y, 1))
    expected = 1
    greet(is_b0 | is_b2, col(y // 2 + 1, 0))
    expected += count(is_a & ((y == 1) | (y == 2)))
    greet(is_b0 | is_b2, col(y // 2, 0))
    expected += count(is_a & (y < 2))
    greet(is_b0, home(0, 0))
    expected += count(is_first_home)
    greet(is_b2, col(3, 0))
    expected += count(is_a3)
    greet(y == 1, col(0, c))
    expected += count(is_a0)
    greet(is_a & ((y == 1) | (y == 2)), col(y + 1, 0))
    greet(is_b0, col(2, 1))
    expected += count((is_a & (y >= 2)) | is_b2)
    greet(is_two, col(1 - c, c))
    expected += count(is_hub)
    greet(is_last, col(1 - c, c))
    expected += count(is_hub)
    greet(is_last, col(2, c))
    expected += count(is_two)
    greet((y == 0) & (x_half == 1), index_of(middle, 0, z, 0))
    expected += count(is_a0)
    greet((y >= 2) | ((y == 1) & (x_half == 1)), index_of(middle, x_half, z, 1 - x_half))
    expected += count(is_hub, 3)
    greet((y == 1) & (x_half == 0), index_of(middle, 1, z, 1))
    expected += count(is_b1)
    greet(y >= 2, producer(x_half, y, middle, z))
    expected += count(is_two) + count(is_last)
    before = jnp.maximum(me - 1, 0)
    bc, bz, bx, by = before % 2, (before // 2) % 8, (before // 16) % 4, before // 64
    first_before = (by == 0) & (bx // 2 == 0)
    greet(
        me >= 1,
        jnp.where(first_before, before, producer(bx // 2, by, middle_x(bx, bc), bz)),
    )
    goes_on = ~(is_a3 & (residue == 31))
    expected += count(is_first_home) + count(is_a0) + count(y == 1) + count(is_two)
    expected += count(is_last & goes_on)

    @pl.when(is_first_home)
    def _():
        pltpu.make_async_copy(through_ref.at[0], W.at[T3], local.at[1]).start()
        pltpu.make_async_copy(reflect_ref.at[0], W.at[P3], local.at[2]).start()

    maps_copy = pltpu.make_async_copy(maps_ref.at[0], maps, local.at[0])
    maps_copy.start()
    pl.semaphore_wait(barrier, expected)

    other = lax.rem(me + 1, lax.axis_size("sec"))

    def message(source, target, s, r, device):
        return pltpu.make_async_remote_copy(
            src_ref=source, dst_ref=target, send_sem=send.at[s], recv_sem=recv.at[r],
            device_id=(device,), device_id_type=MESH,
        )

    finals = []

    def post(condition, source, target, s, r, device):
        @pl.when(condition)
        def _():
            message(source, target, s, r, device).start()

        finals.append((condition, source, s))

    def got(target, r):
        message(target, target, 0, r, other).wait_recv()

    def sent(source, s):
        message(source, source, s, 0, other).wait_send()

    sections = (mirror_ref, reflect_ref, through_ref, back_ref)
    middle_a = index_of(middle, y, z, 0)

    def rows(block, half):
        return W.at[block, pl.ds(half * (M // 2), M // 2)]

    def piece(part, half):
        return sections[part].at[0, pl.ds(half * (M // 2), M // 2)]

    def slot(block, half):
        return 2 * block + half

    def first_send(part, half):
        message(
            piece(part, half), rows(4 * x_half + part, half), 2 * part + half,
            slot(4 * x_half + part, half), middle_a,
        ).start()

    def turned(third):
        return (3, 2) if third else (2, 3)

    def later_send(order, half):
        @pl.when(y == 0)
        def _():
            first_send(turned(order == 2)[0], half)

        @pl.when(y > 0)
        def _():
            first_send(order, half)

    def pass_on(part, half, who):
        @pl.when(who)
        def _():
            got(rows(FQ + part, half), slot(FQ + part, half))
            got(rows(LQ + part, half), slot(LQ + part, half))

        at = 8 + 2 * part + half
        post(who & ((y == 1) | (y == 2)), rows(FQ + part, half), rows(LQ + part, half), at,
             slot(LQ + part, half), col(2 * (y - 1), 1))
        post(who & (y < 2), rows(LQ + part, half), rows(FQ + part, half), at + 8,
             slot(FQ + part, half), col(2 * y, 1))
        post(who & (y == 2), rows(LQ + part, half), rows(DQ + part, half), at + 8,
             slot(8 + part, half), col(2, 1))
        if part in (0, 3):
            first = 0 if part == 0 else 1
            post(who & (y == 0), rows(FQ + part, half), rows(HQ + first, half), at,
                 slot(14 + first, half), col(0, 1))
        else:
            post(who & (y == 3), rows(FQ + part, half), rows(R6 + part - 1, half), at,
                 slot(12 + part - 1, half), col(2, 1))

    def both_halves(block, receive):
        for half in (0, 1):
            got(rows(block, half), slot(receive, half))

    for part in (0, 1):
        for half in (0, 1):
            first_send(part, half)

    @pl.when(is_first_home)
    def _():
        pltpu.make_async_copy(through_ref.at[0], W.at[T3], local.at[1]).wait()
        pltpu.make_async_copy(reflect_ref.at[0], W.at[P3], local.at[2]).wait()
        V[TL] = mm(W[T3], incident_ref[...])
        V[RL] = mm(W[P3], incident_ref[...])

    post(is_first_home, V.at[TL], V.at[HT], 40, 36, index_of(middle, 0, z, 1))
    post(is_first_home, V.at[RL], V.at[HR], 41, 37, index_of(middle, 0, z, 1))
    post(is_first_home, V.at[TL], V.at[ENT], 42, 45, other)

    maps_copy.wait()
    for j in range(DEPTHS):
        maps_left[j * M : (j + 1) * M, :] = left(maps[j])

    for part in (0, 1):
        for half in (0, 1):
            pass_on(part, half, is_a)
            sent(piece(part, half), 2 * part + half)
            later_send(part + 2, half)

    @pl.when(is_mid)
    def _():
        @pl.when(c == 1)
        def _():
            for part in (0, 1):
                both_halves(FQ + part, FQ + part)
                both_halves(LQ + part, LQ + part)

        bounce, both = spread(W[FQ], W[LR])
        W[TX] = bounce
        W[TM] = both

    for half in (0, 1):
        pass_on(2, half, is_a & (y > 0))
        pass_on(3, half, is_a0)

    @pl.when(is_a0)
    def _():
        partial_value, full_value = summed(W[TX], W[TM], mm(W[FQ], W[LU]))
        W[TRP] = full_value
        W[CU] = mm(W[FU], W[LU] + mm(W[LR], partial_value))

    post(is_a0, W.at[CU], W.at[HU], 27, 35, col(1, 0))

    @pl.when(is_mid & ~is_a0)
    def _():
        @pl.when(c == 1)
        def _():
            both_halves(FT, FT)
            both_halves(LT, LT)

        g_through = summed(W[TX], W[TM], W[FT])[1]
        W[CT] = mm(W[LT], g_through)
        W[TRP] = mm(W[LR], g_through)

    @pl.when(is_b2)
    def _():
        for part in (0, 1, 2):
            both_halves(DQ + part, 8 + part)
        both_halves(R6, 12)
        bounce, both = spread(W[DQ], W[R6])
        W[P3] = summed(bounce, both, W[DT])[1]
        W[T3] = mm(W[R6], W[P3])
        both_halves(DU, 11)
        W[RIN] = W[DR] + mm(W[DU], W[T3])

    for half in (0, 1):
        pass_on(3, half, is_a & (y > 0))

        @pl.when(is_mid & ~is_a0)
        def _(half=half):
            here = pl.ds(half * (M // 2), M // 2)

            @pl.when(c == 1)
            def _():
                got(rows(FU, half), slot(FU, half))
                got(rows(LU, half), slot(LU, half))

            W[CR, here] = W[FR, here] + mm(W[FU, here], W[TRP])

        post((is_a & (y >= 2)) | is_b2, rows(CR, half), rows(RIN, half), 24 + 20 * half, 38 + 10 * half,
             jnp.where(is_a, col(y - 1, 0), col(0, 1)))

    for half in (0, 1):
        pass_on(2, half, is_a0)

    @pl.when(is_a0)
    def _():
        W[CQ] = W[LQ] + mm(W[LT], W[TRP])

    post(is_a0, W.at[CQ], W.at[HQ], 26, 34, col(1, 0))

    @pl.when(is_a0)
    def _():
        value = summed(W[TX], W[TM], mm(W[FT], incident_ref[...]))[1]
        V[T01] = mm(W[LT], value)
        V[R01] = mm(W[FR], incident_ref[...]) + mm(W[FU], mm(W[LR], value))

    @pl.when(is_mid & ~is_a0)
    def _():
        partial_value, full_value = summed(W[TX], W[TM], mm(W[FQ], W[LU]))
        W[CQ] = W[LQ] + mm(W[LT], full_value)
        W[CU] = mm(W[FU], W[LU] + mm(W[LR], partial_value))

    post(is_a0, V.at[T01], V.at[HT], 28, 36, col(1, 0))
    post(is_a0, V.at[R01], V.at[HR], 29, 37, col(1, 0))
    post(is_a0, V.at[pl.ds(T01, 2)], V.at[pl.ds(TL, 2)], 30, 43, home(0, 1))
    post(is_a0, V.at[T01], V.at[ENT], 31, 45, 32 + residue + 1)

    def turn(step, carry):
        @pl.when((is_hub | is_two) & (step == 2 * c))
        def _():
            @pl.when(~is_b2)
            def _():
                got(rows(RIN, 0), 38)
                got(rows(RIN, 1), 48)

            bounce, both = spread(W[CQ], W[RIN])
            W[POUT] = summed(bounce, both, W[CT])[1]
            W[TRP] = mm(W[RIN], W[POUT])
            for half in (0, 1):
                here = pl.ds(half * (M // 2), M // 2)
                W[ROUT, here] = W[CR, here] + mm(W[CU, here], W[TRP])

                @pl.when(is_two)
                def _(half=half):
                    message(rows(ROUT, half), rows(R23, half), 25 + 18 * half, 39 + 8 * half,
                            col(1 - c, c)).start()

            @pl.when(is_a2)
            def _():
                message(W.at[POUT], W.at[POUT], 32, 40, col(3, 0)).start()

        @pl.when(is_hub & (step == 1))
        def _():
            @pl.when(is_a)
            def _():
                got(W.at[HQ], 34)

            @pl.when(c == 1)
            def _():
                both_halves(HQ, 14)

            bounce, both = spread(W[HQ], W[CR])
            W[TX] = bounce
            W[TM] = both
            W[TRP] = mm(W[HQ], W[CU])
            got(V.at[HT], 36)
            value = jnp.concatenate([V[HT], W[TRP]], axis=1)
            partial_value, full_value = summed(W[TX], W[TM], value)
            through = mm(W[CT], full_value)
            V[T01] = through[:, :INC]
            W[Q01] = W[CQ] + through[:, INC:]
            back = mm(W[CR], jnp.concatenate([full_value[:, :INC], partial_value[:, INC:]], axis=1))
            V[G2] = back[:, :INC]
            W[TRP] = W[CU] + back[:, INC:]

            @pl.when(is_a)
            def _():
                got(W.at[HU], 35)

            @pl.when(c == 1)
            def _():
                both_halves(HU, 15)

            returned = mm(W[HU], jnp.concatenate([V[G2], W[TRP]], axis=1))
            W[U01] = returned[:, INC:]
            got(V.at[HR], 37)
            V[R01] = V[HR] + returned[:, :INC]

            @pl.when(is_a)
            def _():
                message(V.at[pl.ds(T01, 2)], V.at[pl.ds(TL, 2)], 30, 43, home(1, 1)).start()
                message(V.at[T01], V.at[ENT], 31, 45, 32 * 3 + residue + 1).start()

            @pl.when(c == 1)
            def _():
                message(V.at[pl.ds(T01, 2)], V.at[pl.ds(T01, 2)], 30, 46, col(1, 1)).start()

        return carry

    lax.fori_loop(0, 3, turn, 0)
    finals.append((is_two, rows(ROUT, 0), 25))
    finals.append((is_two, rows(ROUT, 1), 43))
    finals.append((is_a2, W.at[POUT], 32))
    finals.append((is_hub, V.at[pl.ds(T01, 2)], 30))
    finals.append((is_a1, V.at[T01], 31))

    @pl.when(is_b1)
    def _():
        got(V.at[pl.ds(T01, 2)], 46)

    post(is_b1, V.at[pl.ds(T01, 2)], V.at[pl.ds(TL, 2)], 30, 43, home(1, 0))
    post(is_b1, V.at[T01], V.at[ENT], 31, 45, 32 * 2 + residue + 1)

    @pl.when(is_b2)
    def _():
        both_halves(T6, 13)
        W[T3] = mm(W[T6], mm(W[P3], W[POUT]))

    post(is_b2, W.at[T3], W.at[T3], 32, 40, col(3, 1))

    def stack_field():
        message(V.at[G3], V.at[GL], 33, 42, col(3, c)).start()

    def step_field():
        message(V.at[P1], V.at[PL], 34, 41, col(2, c)).start()

    def early_reflected():
        V[RB] = V[HR] + mm(W[HU], mm(W[ROUT], V[G2]))
        message(V.at[RB], V.at[RL], 36, 44, home(2, chain_half)).start()

    def late_reflected():
        V[RC] = V[R01] + mm(W[U01], mm(W[R23], V[G3]))
        message(V.at[RC], V.at[RL], 35, 44, home(3, chain_half)).start()

    def arrived():
        got(rows(R23, 0), 39)
        got(rows(R23, 1), 47)

    @pl.when(is_a1)
    def _():
        arrived()
        late, early = mm(W[Q01], W[R23]), mm(W[HQ], W[ROUT])
        late_value, early_value = V[T01], V[HT]
        for _ in range(3):
            late_value = V[T01] + mm(late, late_value)
            early_value = V[HT] + mm(early, early_value)
        V[G3] = late_value
        V[G2] = early_value
        stack_field()
        V[P1] = mm(W[POUT], early_value)
        step_field()
        late_reflected()
        early_reflected()

    @pl.when(is_b0)
    def _():
        V[G2] = bounced(mm(W[HQ], W[ROUT]), V[HT])
        V[P1] = mm(W[POUT], V[G2])
        step_field()
        early_reflected()
        arrived()
        V[G3] = bounced(mm(W[Q01], W[R23]), V[T01])
        stack_field()
        late_reflected()

    finals.append((is_hub, V.at[P1], 34))
    finals.append((is_hub, V.at[RB], 36))
    finals.append((is_hub, V.at[G3], 33))
    finals.append((is_hub, V.at[RC], 35))

    @pl.when(is_a3)
    def _():
        got(W.at[POUT], 40)
        W[T3] = mm(W[CT], W[POUT])

    @pl.when(is_last & (c == 1))
    def _():
        got(W.at[T3], 40)

    @pl.when(is_two)
    def _():
        got(V.at[PL], 41)
        V[TA] = mm(W[CT], V[PL])

    post(is_two, V.at[TA], V.at[ENT], 31, 45, 32 * (4 + chain_half) + residue + 1)
    post(is_two, V.at[TA], V.at[TL], 30, 43, home(2, chain_half))

    @pl.when(is_last)
    def _():
        got(V.at[GL], 42)
        V[TB] = mm(W[T3], V[GL])

    post(is_last & goes_on, V.at[TB], V.at[ENT], 38, 45, 32 * (6 + chain_half) + residue + 1)
    post(is_last, V.at[TB], V.at[TL], 37, 43, home(3, chain_half))

    @pl.when((y < 2) & ~is_first_home)
    def _():
        got(V.at[pl.ds(TL, 2)], 43)

    @pl.when(y >= 2)
    def _():
        got(V.at[TL], 43)
        got(V.at[RL], 44)

    through_copy = pltpu.make_async_copy(V.at[TL], through_out.at[0], local.at[3])
    reflected_copy = pltpu.make_async_copy(V.at[RL], reflected_out.at[0], local.at[4])
    through_copy.start()
    reflected_copy.start()

    @pl.when(me >= 1)
    def _():
        got(V.at[ENT], 45)

    @pl.when(me == 0)
    def _():
        V[ENT] = incident_ref[...]

    depth[...] = jnp.dot(maps_left[...], right(V[ENT]), preferred_element_type=F32).reshape(
        DEPTHS, M, INC
    )
    depth_copy = pltpu.make_async_copy(depth, depth_out.at[0], local.at[5])
    depth_copy.start()

    for part in (2, 3):
        for half in (0, 1):
            sent(piece(part, half), 2 * part + half)
    for condition, source, s in finals:
        @pl.when(condition)
        def _(source=source, s=s):
            sent(source, s)

    through_copy.wait()
    reflected_copy.wait()
    depth_copy.wait()


def results_kernel(through_ref, reflected_ref, depth_ref, through_out, reflected_out, depth_out,
                   held, inward, outward):
    pieces = [(through_ref.at[0], through_out.at[0]), (reflected_ref.at[0], reflected_out.at[0])]
    pieces += [(depth_ref.at[0, j], depth_out.at[0, j]) for j in range(DEPTHS)]
    arriving = [
        pltpu.make_async_copy(source, held.at[i], inward.at[i]) for i, (source, _) in enumerate(pieces)
    ]
    leaving = [
        pltpu.make_async_copy(held.at[i], target, outward.at[i]) for i, (_, target) in enumerate(pieces)
    ]
    for copy in arriving:
        copy.start()
    for copy, after in zip(arriving, leaving):
        copy.wait()
        after.start()
    for copy in leaving:
        copy.wait()


def per_device(front_reflect, front_through, back_reflect, back_through, depth_maps, incident):
    anywhere = pl.BlockSpec(memory_space=pl.ANY)
    results = (
        jax.ShapeDtypeStruct((1, M, INC), F32),
        jax.ShapeDtypeStruct((1, M, INC), F32),
        jax.ShapeDtypeStruct((1, DEPTHS, M, INC), F32),
    )
    made = pl.pallas_call(
        kernel,
        out_shape=results,
        in_specs=[anywhere] * 5 + [pl.BlockSpec(memory_space=pltpu.VMEM)],
        out_specs=(anywhere,) * 3,
        scratch_shapes=[
            pltpu.VMEM((BLOCKS, M, M), F32),
            pltpu.VMEM((VECS, M, INC), F32),
            pltpu.VMEM((DEPTHS, M, M), F32),
            pltpu.VMEM((DEPTHS * M, 3 * M), BF16),
            pltpu.VMEM((DEPTHS, M, INC), F32),
            pltpu.SemaphoreType.DMA((45,)),
            pltpu.SemaphoreType.DMA((49,)),
            pltpu.SemaphoreType.DMA((6,)),
        ],
        compiler_params=pltpu.CompilerParams(
            collective_id=0, has_side_effects=True, vmem_limit_bytes=60 * 2**20
        ),
        name="chains",
    )(front_reflect, front_through, back_reflect, back_through, depth_maps, incident)
    return pl.pallas_call(
        results_kernel,
        out_shape=results,
        in_specs=[anywhere] * 3,
        out_specs=(anywhere,) * 3,
        scratch_shapes=[
            pltpu.VMEM((2 + DEPTHS, M, INC), F32),
            pltpu.SemaphoreType.DMA((2 + DEPTHS,)),
            pltpu.SemaphoreType.DMA((2 + DEPTHS,)),
        ],
        compiler_params=pltpu.CompilerParams(vmem_limit_bytes=60 * 2**20),
        name="results",
    )(*made)


def solution(mesh):
    in_specs = (
        P("sec", None, None),
        P("sec", None, None),
        P("sec", None, None),
        P("sec", None, None),
        P("sec", None, None, None),
        P(),
    )
    out_specs = (P("sec", None, None), P("sec", None, None), P("sec", None, None, None))
    return jax.shard_map(
        per_device, mesh=mesh, in_specs=in_specs, out_specs=out_specs, check_vma=False
    )
```

```python
import functools

import jax
import jax.numpy as jnp
from jax import lax
from jax.experimental import pallas as pl
from jax.experimental.pallas import tpu as pltpu
from jax.sharding import PartitionSpec as P


F32, BF16 = jnp.float32, jnp.bfloat16
MESH = pl.DeviceIdType.MESH
M, INC, DEPTHS = 384, 128, 4

FQ, FR, FT, FU, LQ, LR, LT, LU = range(8)
CQ, CR, CT, CU = range(8, 12)
DQ, DR, DT, DU, R6, T6 = range(12, 18)
HQ, HU, RIN, ROUT, POUT, R23, Q01, U01, T3, P3, TX, TM, TRP = range(18, 31)
BLOCKS = 31
HT, HR, T01, R01, G2, G3, P1, RB, RC, TA, TB, PL, GL, TL, RL, ENT = range(16)
VECS = 16


def halves(x):
    high = x.astype(BF16)
    return high, (x - high.astype(F32)).astype(BF16)


def left(x):
    high, low = halves(x)
    return jnp.concatenate([high, low, high], axis=1)


def right(x):
    high, low = halves(x)
    return jnp.concatenate([high, high, low], axis=0)


def mm(a, b):
    return jnp.dot(left(a), right(b), preferred_element_type=F32)


def spread(mirror, reflect):
    bounce = mm(mirror, reflect)
    return bounce, bounce + mm(bounce, bounce)


def summed(bounce, both, value):
    partial_value = value + mm(both, value)
    return partial_value, value + mm(bounce, partial_value)


def bounced(bounce, field):
    value = field
    for _ in range(3):
        value = field + mm(bounce, value)
    return value


def index_of(x, y, z, c):
    return ((y * 4 + x) * 8 + z) * 2 + c


def middle_x(x, c):
    return lax.rem(x + jnp.where(x // 2 == c, 1, 3), 4)


def producer(k_half, y, middle, z):
    return index_of(middle, y, z, 1 - k_half)


def kernel(
    reflect_ref, through_ref, mirror_ref, back_ref, maps_ref, incident_ref,
    through_out, reflected_out, depth_out,
    W, V, maps, maps_left, depth, send, recv, local,
):
    me = lax.axis_index("sec")
    c, z, x, y = me % 2, (me // 2) % 8, (me // 16) % 4, me // 64
    x_half = x // 2
    middle = middle_x(x, c)
    base = 1 - x % 2
    group_c = jnp.where(x % 2 == 1, x_half, 1 - x_half)
    residue = base * 16 + z * 2 + group_c
    chain_half = 1 - c

    def col(at_y, at_c):
        return index_of(x, at_y, z, at_c)

    def home(at_y, half):
        return index_of(base + 2 * half, at_y, z, group_c)

    is_a = c == 0
    is_mid = is_a | (y == 0) | (y == 2)
    is_hub = (is_a & (y == 1)) | ((c == 1) & (y == 0))
    is_two = y == 2
    is_a0, is_a2, is_a3 = is_a & (y == 0), is_a & (y == 2), is_a & (y == 3)
    is_b0, is_b2 = (c == 1) & (y == 0), (c == 1) & (y == 2)
    is_a1, is_b1 = is_a & (y == 1), (c == 1) & (y == 1)
    is_last = y == 3
    is_first_home = (x_half == 0) & (y == 0)

    barrier = pltpu.get_barrier_semaphore()

    def greet(condition, device):
        @pl.when(condition)
        def _():
            pl.semaphore_signal(barrier, inc=1, device_id=(device,), device_id_type=MESH)

    def count(condition, n=1):
        return jnp.where(condition, n, 0)

    greet(is_a, home(y, 0))
    greet(is_a, home(y, 1))
    expected = 1
    greet(is_b0 | is_b2, col(y // 2 + 1, 0))
    expected += count(is_a & ((y == 1) | (y == 2)))
    greet(is_b0 | is_b2, col(y // 2, 0))
    expected += count(is_a & (y < 2))
    greet(is_b0, home(0, 0))
    expected += count(is_first_home)
    greet(is_b2, col(3, 0))
    expected += count(is_a3)
    greet(y == 1, col(0, c))
    expected += count(is_a0)
    greet(is_a & ((y == 1) | (y == 2)), col(y + 1, 0))
    greet(is_b0, col(2, 1))
    expected += count((is_a & (y >= 2)) | is_b2)
    greet(is_two, col(1 - c, c))
    expected += count(is_hub)
    greet(is_last, col(1 - c, c))
    expected += count(is_hub)
    greet(is_last, col(2, c))
    expected += count(is_two)
    greet((y == 0) & (x_half == 1), index_of(middle, 0, z, 0))
    expected += count(is_a0)
    greet((y >= 2) | ((y == 1) & (x_half == 1)), index_of(middle, x_half, z, 1 - x_half))
    expected += count(is_hub, 3)
    greet((y == 1) & (x_half == 0), index_of(middle, 1, z, 1))
    expected += count(is_b1)
    greet(y >= 2, producer(x_half, y, middle, z))
    expected += count(is_two) + count(is_last)
    before = jnp.maximum(me - 1, 0)
    bc, bz, bx, by = before % 2, (before // 2) % 8, (before // 16) % 4, before // 64
    first_before = (by == 0) & (bx // 2 == 0)
    greet(
        me >= 1,
        jnp.where(first_before, before, producer(bx // 2, by, middle_x(bx, bc), bz)),
    )
    goes_on = ~(is_a3 & (residue == 31))
    expected += count(is_first_home) + count(is_a0) + count(y == 1) + count(is_two)
    expected += count(is_last & goes_on)

    @pl.when(is_first_home)
    def _():
        pltpu.make_async_copy(through_ref.at[0], W.at[T3], local.at[1]).start()
        pltpu.make_async_copy(reflect_ref.at[0], W.at[P3], local.at[2]).start()

    maps_copy = pltpu.make_async_copy(maps_ref.at[0], maps, local.at[0])
    maps_copy.start()
    pl.semaphore_wait(barrier, expected)

    other = lax.rem(me + 1, lax.axis_size("sec"))

    def message(source, target, s, r, device):
        return pltpu.make_async_remote_copy(
            src_ref=source, dst_ref=target, send_sem=send.at[s], recv_sem=recv.at[r],
            device_id=(device,), device_id_type=MESH,
        )

    finals = []

    def post(condition, source, target, s, r, device):
        @pl.when(condition)
        def _():
            message(source, target, s, r, device).start()

        finals.append((condition, source, s))

    def got(target, r):
        message(target, target, 0, r, other).wait_recv()

    def sent(source, s):
        message(source, source, s, 0, other).wait_send()

    sections = (mirror_ref, reflect_ref, through_ref, back_ref)
    middle_a = index_of(middle, y, z, 0)

    def rows(block, half):
        return W.at[block, pl.ds(half * (M // 2), M // 2)]

    def piece(part, half):
        return sections[part].at[0, pl.ds(half * (M // 2), M // 2)]

    def slot(block, half):
        return 2 * block + half

    def first_send(part, half):
        message(
            piece(part, half), rows(4 * x_half + part, half), 2 * part + half,
            slot(4 * x_half + part, half), middle_a,
        ).start()

    def turned(third):
        return (3, 2) if third else (2, 3)

    def later_send(order, half):
        @pl.when(y == 0)
        def _():
            first_send(turned(order == 2)[0], half)

        @pl.when(y > 0)
        def _():
            first_send(order, half)

    def pass_on(part, half, who):
        @pl.when(who)
        def _():
            got(rows(FQ + part, half), slot(FQ + part, half))
            got(rows(LQ + part, half), slot(LQ + part, half))

        at = 8 + 2 * part + half
        post(who & ((y == 1) | (y == 2)), rows(FQ + part, half), rows(LQ + part, half), at,
             slot(LQ + part, half), col(2 * (y - 1), 1))
        post(who & (y < 2), rows(LQ + part, half), rows(FQ + part, half), at + 8,
             slot(FQ + part, half), col(2 * y, 1))
        post(who & (y == 2), rows(LQ + part, half), rows(DQ + part, half), at + 8,
             slot(8 + part, half), col(2, 1))
        if part in (0, 3):
            first = 0 if part == 0 else 1
            post(who & (y == 0), rows(FQ + part, half), rows(HQ + first, half), at,
                 slot(14 + first, half), col(0, 1))
        else:
            post(who & (y == 3), rows(FQ + part, half), rows(R6 + part - 1, half), at,
                 slot(12 + part - 1, half), col(2, 1))

    def both_halves(block, receive):
        for half in (0, 1):
            got(rows(block, half), slot(receive, half))

    for part in (0, 1):
        for half in (0, 1):
            first_send(part, half)

    @pl.when(is_first_home)
    def _():
        pltpu.make_async_copy(through_ref.at[0], W.at[T3], local.at[1]).wait()
        pltpu.make_async_copy(reflect_ref.at[0], W.at[P3], local.at[2]).wait()
        V[TL] = mm(W[T3], incident_ref[...])
        V[RL] = mm(W[P3], incident_ref[...])

    post(is_first_home, V.at[TL], V.at[HT], 40, 36, index_of(middle, 0, z, 1))
    post(is_first_home, V.at[RL], V.at[HR], 41, 37, index_of(middle, 0, z, 1))
    post(is_first_home, V.at[TL], V.at[ENT], 42, 45, other)

    maps_copy.wait()
    for j in range(DEPTHS):
        maps_left[j * M : (j + 1) * M, :] = left(maps[j])

    for part in (0, 1):
        for half in (0, 1):
            pass_on(part, half, is_a)
            sent(piece(part, half), 2 * part + half)
            later_send(part + 2, half)

    @pl.when(is_mid)
    def _():
        @pl.when(c == 1)
        def _():
            for part in (0, 1):
                both_halves(FQ + part, FQ + part)
                both_halves(LQ + part, LQ + part)

        bounce, both = spread(W[FQ], W[LR])
        W[TX] = bounce
        W[TM] = both

    for half in (0, 1):
        pass_on(2, half, is_a & (y > 0))
        pass_on(3, half, is_a0)

    @pl.when(is_a0)
    def _():
        partial_value, full_value = summed(W[TX], W[TM], mm(W[FQ], W[LU]))
        W[TRP] = full_value
        W[CU] = mm(W[FU], W[LU] + mm(W[LR], partial_value))

    post(is_a0, W.at[CU], W.at[HU], 27, 35, col(1, 0))

    @pl.when(is_b2)
    def _():
        for part in (0, 1, 2):
            both_halves(DQ + part, 8 + part)
        both_halves(R6, 12)
        bounce, both = spread(W[DQ], W[R6])
        W[P3] = summed(bounce, both, W[DT])[1]
        W[T3] = mm(W[R6], W[P3])

    @pl.when(is_mid & ~is_a0)
    def _():
        @pl.when(c == 1)
        def _():
            both_halves(FT, FT)
            both_halves(LT, LT)

        g_through = summed(W[TX], W[TM], W[FT])[1]
        W[CT] = mm(W[LT], g_through)
        W[TRP] = mm(W[LR], g_through)

    @pl.when(is_b2)
    def _():
        both_halves(DU, 11)
        W[RIN] = W[DR] + mm(W[DU], W[T3])

    for half in (0, 1):
        pass_on(3, half, is_a & (y > 0))

        @pl.when(is_mid & ~is_a0)
        def _(half=half):
            here = pl.ds(half * (M // 2), M // 2)

            @pl.when(c == 1)
            def _():
                got(rows(FU, half), slot(FU, half))
                got(rows(LU, half), slot(LU, half))

            W[CR, here] = W[FR, here] + mm(W[FU, here], W[TRP])

        post((is_a & (y >= 2)) | is_b2, rows(CR, half), rows(RIN, half), 24 + 20 * half, 38 + 10 * half,
             jnp.where(is_a, col(y - 1, 0), col(0, 1)))

    for half in (0, 1):
        pass_on(2, half, is_a0)

    @pl.when(is_a0)
    def _():
        W[CQ] = W[LQ] + mm(W[LT], W[TRP])

    post(is_a0, W.at[CQ], W.at[HQ], 26, 34, col(1, 0))

    @pl.when(is_a0)
    def _():
        value = summed(W[TX], W[TM], mm(W[FT], incident_ref[...]))[1]
        V[T01] = mm(W[LT], value)
        V[R01] = mm(W[FR], incident_ref[...]) + mm(W[FU], mm(W[LR], value))

    @pl.when(is_mid & ~is_a0)
    def _():
        partial_value, full_value = summed(W[TX], W[TM], mm(W[FQ], W[LU]))
        W[CQ] = W[LQ] + mm(W[LT], full_value)
        W[CU] = mm(W[FU], W[LU] + mm(W[LR], partial_value))

    post(is_a0, V.at[T01], V.at[HT], 28, 36, col(1, 0))
    post(is_a0, V.at[R01], V.at[HR], 29, 37, col(1, 0))
    post(is_a0, V.at[pl.ds(T01, 2)], V.at[pl.ds(TL, 2)], 30, 43, home(0, 1))
    post(is_a0, V.at[T01], V.at[ENT], 31, 45, 32 + residue + 1)

    def turn(step, carry):
        @pl.when((is_hub | is_two) & (step == 2 * c))
        def _():
            @pl.when(~is_b2)
            def _():
                got(rows(RIN, 0), 38)
                got(rows(RIN, 1), 48)

            bounce, both = spread(W[CQ], W[RIN])
            W[POUT] = summed(bounce, both, W[CT])[1]
            W[TRP] = mm(W[RIN], W[POUT])
            for half in (0, 1):
                here = pl.ds(half * (M // 2), M // 2)
                W[ROUT, here] = W[CR, here] + mm(W[CU, here], W[TRP])

                @pl.when(is_two)
                def _(half=half):
                    message(rows(ROUT, half), rows(R23, half), 25 + 18 * half, 39 + 8 * half,
                            col(1 - c, c)).start()

            @pl.when(is_a2)
            def _():
                message(W.at[POUT], W.at[POUT], 32, 40, col(3, 0)).start()

        @pl.when(is_hub & (step == 1))
        def _():
            @pl.when(is_a)
            def _():
                got(W.at[HQ], 34)

            @pl.when(c == 1)
            def _():
                both_halves(HQ, 14)

            bounce, both = spread(W[HQ], W[CR])
            W[TX] = bounce
            W[TM] = both
            W[TRP] = mm(W[HQ], W[CU])
            got(V.at[HT], 36)
            value = jnp.concatenate([V[HT], W[TRP]], axis=1)
            partial_value, full_value = summed(W[TX], W[TM], value)
            through = mm(W[CT], full_value)
            V[T01] = through[:, :INC]
            W[Q01] = W[CQ] + through[:, INC:]
            back = mm(W[CR], jnp.concatenate([full_value[:, :INC], partial_value[:, INC:]], axis=1))
            V[G2] = back[:, :INC]
            W[TRP] = W[CU] + back[:, INC:]

            @pl.when(is_a)
            def _():
                got(W.at[HU], 35)

            @pl.when(c == 1)
            def _():
                both_halves(HU, 15)

            returned = mm(W[HU], jnp.concatenate([V[G2], W[TRP]], axis=1))
            W[U01] = returned[:, INC:]
            got(V.at[HR], 37)
            V[R01] = V[HR] + returned[:, :INC]

            @pl.when(is_a)
            def _():
                message(V.at[pl.ds(T01, 2)], V.at[pl.ds(TL, 2)], 30, 43, home(1, 1)).start()
                message(V.at[T01], V.at[ENT], 31, 45, 32 * 3 + residue + 1).start()

            @pl.when(c == 1)
            def _():
                message(V.at[pl.ds(T01, 2)], V.at[pl.ds(T01, 2)], 30, 46, col(1, 1)).start()

        return carry

    lax.fori_loop(0, 3, turn, 0)
    finals.append((is_two, rows(ROUT, 0), 25))
    finals.append((is_two, rows(ROUT, 1), 43))
    finals.append((is_a2, W.at[POUT], 32))
    finals.append((is_hub, V.at[pl.ds(T01, 2)], 30))
    finals.append((is_a1, V.at[T01], 31))

    @pl.when(is_b1)
    def _():
        got(V.at[pl.ds(T01, 2)], 46)

    post(is_b1, V.at[pl.ds(T01, 2)], V.at[pl.ds(TL, 2)], 30, 43, home(1, 0))
    post(is_b1, V.at[T01], V.at[ENT], 31, 45, 32 * 2 + residue + 1)

    @pl.when(is_b2)
    def _():
        both_halves(T6, 13)
        W[T3] = mm(W[T6], mm(W[P3], W[POUT]))

    post(is_b2, W.at[T3], W.at[T3], 32, 40, col(3, 1))

    def stack_field():
        message(V.at[G3], V.at[GL], 33, 42, col(3, c)).start()

    def step_field():
        message(V.at[P1], V.at[PL], 34, 41, col(2, c)).start()

    def early_reflected():
        V[RB] = V[HR] + mm(W[HU], mm(W[ROUT], V[G2]))
        message(V.at[RB], V.at[RL], 36, 44, home(2, chain_half)).start()

    def late_reflected():
        V[RC] = V[R01] + mm(W[U01], mm(W[R23], V[G3]))
        message(V.at[RC], V.at[RL], 35, 44, home(3, chain_half)).start()

    def arrived():
        got(rows(R23, 0), 39)
        got(rows(R23, 1), 47)

    @pl.when(is_a1)
    def _():
        arrived()
        late, early = mm(W[Q01], W[R23]), mm(W[HQ], W[ROUT])
        late_value, early_value = V[T01], V[HT]
        for _ in range(3):
            late_value = V[T01] + mm(late, late_value)
            early_value = V[HT] + mm(early, early_value)
        V[G3] = late_value
        V[G2] = early_value
        stack_field()
        V[P1] = mm(W[POUT], early_value)
        step_field()
        late_reflected()
        early_reflected()

    @pl.when(is_b0)
    def _():
        V[G2] = bounced(mm(W[HQ], W[ROUT]), V[HT])
        V[P1] = mm(W[POUT], V[G2])
        step_field()
        early_reflected()
        arrived()
        V[G3] = bounced(mm(W[Q01], W[R23]), V[T01])
        stack_field()
        late_reflected()

    finals.append((is_hub, V.at[P1], 34))
    finals.append((is_hub, V.at[RB], 36))
    finals.append((is_hub, V.at[G3], 33))
    finals.append((is_hub, V.at[RC], 35))

    @pl.when(is_a3)
    def _():
        got(W.at[POUT], 40)
        W[T3] = mm(W[CT], W[POUT])

    @pl.when(is_last & (c == 1))
    def _():
        got(W.at[T3], 40)

    @pl.when(is_two)
    def _():
        got(V.at[PL], 41)
        V[TA] = mm(W[CT], V[PL])

    post(is_two, V.at[TA], V.at[ENT], 31, 45, 32 * (4 + chain_half) + residue + 1)
    post(is_two, V.at[TA], V.at[TL], 30, 43, home(2, chain_half))

    @pl.when(is_last)
    def _():
        got(V.at[GL], 42)
        V[TB] = mm(W[T3], V[GL])

    post(is_last & goes_on, V.at[TB], V.at[ENT], 38, 45, 32 * (6 + chain_half) + residue + 1)
    post(is_last, V.at[TB], V.at[TL], 37, 43, home(3, chain_half))

    @pl.when((y < 2) & ~is_first_home)
    def _():
        got(V.at[pl.ds(TL, 2)], 43)

    @pl.when(y >= 2)
    def _():
        got(V.at[TL], 43)
        got(V.at[RL], 44)

    through_copy = pltpu.make_async_copy(V.at[TL], through_out.at[0], local.at[3])
    reflected_copy = pltpu.make_async_copy(V.at[RL], reflected_out.at[0], local.at[4])
    through_copy.start()
    reflected_copy.start()

    @pl.when(me >= 1)
    def _():
        got(V.at[ENT], 45)

    @pl.when(me == 0)
    def _():
        V[ENT] = incident_ref[...]

    depth[...] = jnp.dot(maps_left[...], right(V[ENT]), preferred_element_type=F32).reshape(
        DEPTHS, M, INC
    )
    depth_copy = pltpu.make_async_copy(depth, depth_out.at[0], local.at[5])
    depth_copy.start()

    for part in (2, 3):
        for half in (0, 1):
            sent(piece(part, half), 2 * part + half)
    for condition, source, s in finals:
        @pl.when(condition)
        def _(source=source, s=s):
            sent(source, s)

    through_copy.wait()
    reflected_copy.wait()
    depth_copy.wait()


def results_kernel(through_ref, reflected_ref, depth_ref, through_out, reflected_out, depth_out,
                   held, inward, outward):
    pieces = [(through_ref.at[0], through_out.at[0]), (reflected_ref.at[0], reflected_out.at[0])]
    pieces += [(depth_ref.at[0, j], depth_out.at[0, j]) for j in range(DEPTHS)]
    arriving = [
        pltpu.make_async_copy(source, held.at[i], inward.at[i]) for i, (source, _) in enumerate(pieces)
    ]
    leaving = [
        pltpu.make_async_copy(held.at[i], target, outward.at[i]) for i, (_, target) in enumerate(pieces)
    ]
    for copy in arriving:
        copy.start()
    for copy, after in zip(arriving, leaving):
        copy.wait()
        after.start()
    for copy in leaving:
        copy.wait()


def per_device(front_reflect, front_through, back_reflect, back_through, depth_maps, incident):
    anywhere = pl.BlockSpec(memory_space=pl.ANY)
    results = (
        jax.ShapeDtypeStruct((1, M, INC), F32),
        jax.ShapeDtypeStruct((1, M, INC), F32),
        jax.ShapeDtypeStruct((1, DEPTHS, M, INC), F32),
    )
    made = pl.pallas_call(
        kernel,
        out_shape=results,
        in_specs=[anywhere] * 5 + [pl.BlockSpec(memory_space=pltpu.VMEM)],
        out_specs=(anywhere,) * 3,
        scratch_shapes=[
            pltpu.VMEM((BLOCKS, M, M), F32),
            pltpu.VMEM((VECS, M, INC), F32),
            pltpu.VMEM((DEPTHS, M, M), F32),
            pltpu.VMEM((DEPTHS * M, 3 * M), BF16),
            pltpu.VMEM((DEPTHS, M, INC), F32),
            pltpu.SemaphoreType.DMA((45,)),
            pltpu.SemaphoreType.DMA((49,)),
            pltpu.SemaphoreType.DMA((6,)),
        ],
        compiler_params=pltpu.CompilerParams(
            collective_id=0, has_side_effects=True, vmem_limit_bytes=60 * 2**20
        ),
        name="chains",
    )(front_reflect, front_through, back_reflect, back_through, depth_maps, incident)
    return pl.pallas_call(
        results_kernel,
        out_shape=results,
        in_specs=[anywhere] * 3,
        out_specs=(anywhere,) * 3,
        scratch_shapes=[
            pltpu.VMEM((2 + DEPTHS, M, INC), F32),
            pltpu.SemaphoreType.DMA((2 + DEPTHS,)),
            pltpu.SemaphoreType.DMA((2 + DEPTHS,)),
        ],
        compiler_params=pltpu.CompilerParams(vmem_limit_bytes=60 * 2**20),
        name="results",
    )(*made)


def solution(mesh):
    in_specs = (
        P("sec", None, None),
        P("sec", None, None),
        P("sec", None, None),
        P("sec", None, None),
        P("sec", None, None, None),
        P(),
    )
    out_specs = (P("sec", None, None), P("sec", None, None), P("sec", None, None, None))
    return jax.shard_map(
        per_device, mesh=mesh, in_specs=in_specs, out_specs=out_specs, check_vma=False
    )
```

```python
import functools

import jax
import jax.numpy as jnp
from jax import lax
from jax.experimental import pallas as pl
from jax.experimental.pallas import tpu as pltpu
from jax.sharding import PartitionSpec as P


F32, BF16 = jnp.float32, jnp.bfloat16
MESH = pl.DeviceIdType.MESH
M, INC, DEPTHS = 384, 128, 4

FQ, FR, FT, FU, LQ, LR, LT, LU = range(8)
CQ, CR, CT, CU = range(8, 12)
DQ, DR, DT, DU, R6, T6 = range(12, 18)
HQ, HU, RIN, ROUT, POUT, R23, Q01, U01, T3, P3, TX, TM, TRP = range(18, 31)
BLOCKS = 31
HT, HR, T01, R01, G2, G3, P1, RB, RC, TA, TB, PL, GL, TL, RL, ENT = range(16)
VECS = 16


def halves(x):
    high = x.astype(BF16)
    return high, (x - high.astype(F32)).astype(BF16)


def left(x):
    high, low = halves(x)
    return jnp.concatenate([high, low, high], axis=1)


def right(x):
    high, low = halves(x)
    return jnp.concatenate([high, high, low], axis=0)


def mm(a, b):
    return jnp.dot(left(a), right(b), preferred_element_type=F32)


def spread(mirror, reflect):
    bounce = mm(mirror, reflect)
    return bounce, bounce + mm(bounce, bounce)


def summed(bounce, both, value):
    partial_value = value + mm(both, value)
    return partial_value, value + mm(bounce, partial_value)


def bounced(bounce, field):
    value = field
    for _ in range(3):
        value = field + mm(bounce, value)
    return value


def index_of(x, y, z, c):
    return ((y * 4 + x) * 8 + z) * 2 + c


def middle_x(x, c):
    return lax.rem(x + jnp.where(x // 2 == c, 1, 3), 4)


def producer(k_half, y, middle, z):
    return index_of(middle, y, z, 1 - k_half)


def kernel(
    reflect_ref, through_ref, mirror_ref, back_ref, maps_ref, incident_ref,
    through_out, reflected_out, depth_out,
    W, V, maps, maps_left, depth, send, recv, local,
):
    me = lax.axis_index("sec")
    c, z, x, y = me % 2, (me // 2) % 8, (me // 16) % 4, me // 64
    x_half = x // 2
    middle = middle_x(x, c)
    base = 1 - x % 2
    group_c = jnp.where(x % 2 == 1, x_half, 1 - x_half)
    residue = base * 16 + z * 2 + group_c
    chain_half = 1 - c

    def col(at_y, at_c):
        return index_of(x, at_y, z, at_c)

    def home(at_y, half):
        return index_of(base + 2 * half, at_y, z, group_c)

    is_a = c == 0
    is_mid = is_a | (y == 0) | (y == 2)
    is_hub = (is_a & (y == 1)) | ((c == 1) & (y == 0))
    is_two = y == 2
    is_a0, is_a2, is_a3 = is_a & (y == 0), is_a & (y == 2), is_a & (y == 3)
    is_b0, is_b2 = (c == 1) & (y == 0), (c == 1) & (y == 2)
    is_a1, is_b1 = is_a & (y == 1), (c == 1) & (y == 1)
    is_last = y == 3
    is_first_home = (x_half == 0) & (y == 0)

    barrier = pltpu.get_barrier_semaphore()

    def greet(condition, device):
        @pl.when(condition)
        def _():
            pl.semaphore_signal(barrier, inc=1, device_id=(device,), device_id_type=MESH)

    def count(condition, n=1):
        return jnp.where(condition, n, 0)

    greet(is_a, home(y, 0))
    greet(is_a, home(y, 1))
    expected = 1
    greet(is_b0 | is_b2, col(y // 2 + 1, 0))
    expected += count(is_a & ((y == 1) | (y == 2)))
    greet(is_b0 | is_b2, col(y // 2, 0))
    expected += count(is_a & (y < 2))
    greet(is_b0, home(0, 0))
    expected += count(is_first_home)
    greet(is_b2, col(3, 0))
    expected += count(is_a3)
    greet(y == 1, col(0, c))
    expected += count(is_a0)
    greet(is_a & ((y == 1) | (y == 2)), col(y + 1, 0))
    greet(is_b0, col(2, 1))
    expected += count((is_a & (y >= 2)) | is_b2)
    greet(is_two, col(1 - c, c))
    expected += count(is_hub)
    greet(is_last, col(1 - c, c))
    expected += count(is_hub)
    greet(is_last, col(2, c))
    expected += count(is_two)
    greet((y == 0) & (x_half == 1), index_of(middle, 0, z, 0))
    expected += count(is_a0)
    greet((y >= 2) | ((y == 1) & (x_half == 1)), index_of(middle, x_half, z, 1 - x_half))
    expected += count(is_hub, 3)
    greet((y == 1) & (x_half == 0), index_of(middle, 1, z, 1))
    expected += count(is_b1)
    greet(y >= 2, producer(x_half, y, middle, z))
    expected += count(is_two) + count(is_last)
    before = jnp.maximum(me - 1, 0)
    bc, bz, bx, by = before % 2, (before // 2) % 8, (before // 16) % 4, before // 64
    first_before = (by == 0) & (bx // 2 == 0)
    greet(
        me >= 1,
        jnp.where(first_before, before, producer(bx // 2, by, middle_x(bx, bc), bz)),
    )
    goes_on = ~(is_a3 & (residue == 31))
    expected += count(is_first_home) + count(is_a0) + count(y == 1) + count(is_two)
    expected += count(is_last & goes_on)

    @pl.when(is_first_home)
    def _():
        pltpu.make_async_copy(through_ref.at[0], W.at[T3], local.at[1]).start()
        pltpu.make_async_copy(reflect_ref.at[0], W.at[P3], local.at[2]).start()

    maps_copy = pltpu.make_async_copy(maps_ref.at[0], maps, local.at[0])
    maps_copy.start()
    pl.semaphore_wait(barrier, expected)

    other = lax.rem(me + 1, lax.axis_size("sec"))

    def message(source, target, s, r, device):
        return pltpu.make_async_remote_copy(
            src_ref=source, dst_ref=target, send_sem=send.at[s], recv_sem=recv.at[r],
            device_id=(device,), device_id_type=MESH,
        )

    finals = []

    def post(condition, source, target, s, r, device):
        @pl.when(condition)
        def _():
            message(source, target, s, r, device).start()

        finals.append((condition, source, s))

    def got(target, r):
        message(target, target, 0, r, other).wait_recv()

    def sent(source, s):
        message(source, source, s, 0, other).wait_send()

    sections = (mirror_ref, reflect_ref, through_ref, back_ref)
    middle_a = index_of(middle, y, z, 0)

    def rows(block, half):
        return W.at[block, pl.ds(half * (M // 2), M // 2)]

    def piece(part, half):
        return sections[part].at[0, pl.ds(half * (M // 2), M // 2)]

    def slot(block, half):
        return 2 * block + half

    def first_send(part, half):
        message(
            piece(part, half), rows(4 * x_half + part, half), 2 * part + half,
            slot(4 * x_half + part, half), middle_a,
        ).start()

    def turned(third):
        return (3, 2) if third else (2, 3)

    def later_send(order, half):
        @pl.when(y == 0)
        def _():
            first_send(turned(order == 2)[0], half)

        @pl.when(y > 0)
        def _():
            first_send(order, half)

    def pass_on(part, half, who):
        @pl.when(who)
        def _():
            got(rows(FQ + part, half), slot(FQ + part, half))
            got(rows(LQ + part, half), slot(LQ + part, half))

        at = 8 + 2 * part + half
        post(who & ((y == 1) | (y == 2)), rows(FQ + part, half), rows(LQ + part, half), at,
             slot(LQ + part, half), col(2 * (y - 1), 1))
        post(who & (y < 2), rows(LQ + part, half), rows(FQ + part, half), at + 8,
             slot(FQ + part, half), col(2 * y, 1))
        post(who & (y == 2), rows(LQ + part, half), rows(DQ + part, half), at + 8,
             slot(8 + part, half), col(2, 1))
        if part in (0, 3):
            first = 0 if part == 0 else 1
            post(who & (y == 0), rows(FQ + part, half), rows(HQ + first, half), at,
                 slot(14 + first, half), col(0, 1))
        else:
            post(who & (y == 3), rows(FQ + part, half), rows(R6 + part - 1, half), at,
                 slot(12 + part - 1, half), col(2, 1))

    def both_halves(block, receive):
        for half in (0, 1):
            got(rows(block, half), slot(receive, half))

    for part in (0, 1):
        for half in (0, 1):
            first_send(part, half)

    @pl.when(is_first_home)
    def _():
        pltpu.make_async_copy(through_ref.at[0], W.at[T3], local.at[1]).wait()
        pltpu.make_async_copy(reflect_ref.at[0], W.at[P3], local.at[2]).wait()
        V[TL] = mm(W[T3], incident_ref[...])
        V[RL] = mm(W[P3], incident_ref[...])

    post(is_first_home, V.at[TL], V.at[HT], 40, 36, index_of(middle, 0, z, 1))
    post(is_first_home, V.at[RL], V.at[HR], 41, 37, index_of(middle, 0, z, 1))
    post(is_first_home, V.at[TL], V.at[ENT], 42, 45, other)

    maps_copy.wait()
    for j in range(DEPTHS):
        maps_left[j * M : (j + 1) * M, :] = left(maps[j])

    for part in (0, 1):
        for half in (0, 1):
            pass_on(part, half, is_a)
            sent(piece(part, half), 2 * part + half)
            later_send(part + 2, half)

    @pl.when(is_mid)
    def _():
        @pl.when(c == 1)
        def _():
            for part in (0, 1):
                both_halves(FQ + part, FQ + part)
                both_halves(LQ + part, LQ + part)

        bounce, both = spread(W[FQ], W[LR])
        W[TX] = bounce
        W[TM] = both

    for half in (0, 1):
        pass_on(2, half, is_a & (y > 0))
        pass_on(3, half, is_a0)

    @pl.when(is_a0)
    def _():
        partial_value, full_value = summed(W[TX], W[TM], mm(W[FQ], W[LU]))
        W[TRP] = full_value
        W[CU] = mm(W[FU], W[LU] + mm(W[LR], partial_value))

    post(is_a0, W.at[CU], W.at[HU], 27, 35, col(1, 0))

    @pl.when(is_b2)
    def _():
        for part in (0, 1, 2):
            both_halves(DQ + part, 8 + part)
        both_halves(R6, 12)
        bounce, both = spread(W[DQ], W[R6])
        W[P3] = summed(bounce, both, W[DT])[1]
        W[T3] = mm(W[R6], W[P3])

    @pl.when(is_mid & ~is_a0)
    def _():
        @pl.when(c == 1)
        def _():
            both_halves(FT, FT)
            both_halves(LT, LT)

        g_through = summed(W[TX], W[TM], W[FT])[1]
        W[CT] = mm(W[LT], g_through)
        W[TRP] = mm(W[LR], g_through)

    @pl.when(is_b2)
    def _():
        both_halves(DU, 11)
        W[RIN] = W[DR] + mm(W[DU], W[T3])

    for half in (0, 1):
        pass_on(3, half, is_a & (y > 0))

        @pl.when(is_mid & ~is_a0)
        def _(half=half):
            here = pl.ds(half * (M // 2), M // 2)

            @pl.when(c == 1)
            def _():
                got(rows(FU, half), slot(FU, half))
                got(rows(LU, half), slot(LU, half))

            W[CR, here] = W[FR, here] + mm(W[FU, here], W[TRP])

        post((is_a & (y >= 2)) | is_b2, rows(CR, half), rows(RIN, half), 24 + 20 * half, 38 + 10 * half,
             jnp.where(is_a, col(y - 1, 0), col(0, 1)))

    for half in (0, 1):
        pass_on(2, half, is_a0)

    @pl.when(is_a0)
    def _():
        W[CQ] = W[LQ] + mm(W[LT], W[TRP])

    post(is_a0, W.at[CQ], W.at[HQ], 26, 34, col(1, 0))

    @pl.when(is_a0)
    def _():
        value = summed(W[TX], W[TM], mm(W[FT], incident_ref[...]))[1]
        V[T01] = mm(W[LT], value)
        V[R01] = mm(W[FR], incident_ref[...]) + mm(W[FU], mm(W[LR], value))

    @pl.when(is_mid & ~is_a0)
    def _():
        partial_value, full_value = summed(W[TX], W[TM], mm(W[FQ], W[LU]))
        W[CQ] = W[LQ] + mm(W[LT], full_value)
        W[CU] = mm(W[FU], W[LU] + mm(W[LR], partial_value))

    post(is_a0, V.at[T01], V.at[HT], 28, 36, col(1, 0))
    post(is_a0, V.at[R01], V.at[HR], 29, 37, col(1, 0))
    post(is_a0, V.at[pl.ds(T01, 2)], V.at[pl.ds(TL, 2)], 30, 43, home(0, 1))
    post(is_a0, V.at[T01], V.at[ENT], 31, 45, 32 + residue + 1)

    def turn(step, carry):
        @pl.when((is_hub | is_two) & (step == 2 * c))
        def _():
            @pl.when(~is_b2)
            def _():
                got(rows(RIN, 0), 38)
                got(rows(RIN, 1), 48)

            bounce, both = spread(W[CQ], W[RIN])
            W[POUT] = summed(bounce, both, W[CT])[1]
            W[TRP] = mm(W[RIN], W[POUT])
            for half in (0, 1):
                here = pl.ds(half * (M // 2), M // 2)
                W[ROUT, here] = W[CR, here] + mm(W[CU, here], W[TRP])

                @pl.when(is_two)
                def _(half=half):
                    message(rows(ROUT, half), rows(R23, half), 25 + 18 * half, 39 + 8 * half,
                            col(1 - c, c)).start()

            @pl.when(is_a2)
            def _():
                message(W.at[POUT], W.at[POUT], 32, 40, col(3, 0)).start()

        @pl.when(is_hub & (step == 1))
        def _():
            @pl.when(is_a)
            def _():
                got(W.at[HQ], 34)

            @pl.when(c == 1)
            def _():
                both_halves(HQ, 14)

            bounce, both = spread(W[HQ], W[CR])
            W[TX] = bounce
            W[TM] = both
            W[TRP] = mm(W[HQ], W[CU])
            got(V.at[HT], 36)
            value = jnp.concatenate([V[HT], W[TRP]], axis=1)
            partial_value, full_value = summed(W[TX], W[TM], value)
            through = mm(W[CT], full_value)
            V[T01] = through[:, :INC]
            W[Q01] = W[CQ] + through[:, INC:]
            back = mm(W[CR], jnp.concatenate([full_value[:, :INC], partial_value[:, INC:]], axis=1))
            V[G2] = back[:, :INC]
            W[TRP] = W[CU] + back[:, INC:]

            @pl.when(is_a)
            def _():
                got(W.at[HU], 35)

            @pl.when(c == 1)
            def _():
                both_halves(HU, 15)

            returned = mm(W[HU], jnp.concatenate([V[G2], W[TRP]], axis=1))
            W[U01] = returned[:, INC:]
            got(V.at[HR], 37)
            V[R01] = V[HR] + returned[:, :INC]

            @pl.when(is_a)
            def _():
                message(V.at[pl.ds(T01, 2)], V.at[pl.ds(TL, 2)], 30, 43, home(1, 1)).start()
                message(V.at[T01], V.at[ENT], 31, 45, 32 * 3 + residue + 1).start()

            @pl.when(c == 1)
            def _():
                message(V.at[pl.ds(T01, 2)], V.at[pl.ds(T01, 2)], 30, 46, col(1, 1)).start()

        return carry

    lax.fori_loop(0, 3, turn, 0)
    finals.append((is_two, rows(ROUT, 0), 25))
    finals.append((is_two, rows(ROUT, 1), 43))
    finals.append((is_a2, W.at[POUT], 32))
    finals.append((is_hub, V.at[pl.ds(T01, 2)], 30))
    finals.append((is_a1, V.at[T01], 31))

    @pl.when(is_b1)
    def _():
        got(V.at[pl.ds(T01, 2)], 46)

    post(is_b1, V.at[pl.ds(T01, 2)], V.at[pl.ds(TL, 2)], 30, 43, home(1, 0))
    post(is_b1, V.at[T01], V.at[ENT], 31, 45, 32 * 2 + residue + 1)

    @pl.when(is_b2)
    def _():
        both_halves(T6, 13)
        W[T3] = mm(W[T6], mm(W[P3], W[POUT]))

    post(is_b2, W.at[T3], W.at[T3], 32, 40, col(3, 1))

    def stack_field():
        message(V.at[G3], V.at[GL], 33, 42, col(3, c)).start()

    def step_field():
        message(V.at[P1], V.at[PL], 34, 41, col(2, c)).start()

    def early_reflected():
        V[RB] = V[HR] + mm(W[HU], mm(W[ROUT], V[G2]))
        message(V.at[RB], V.at[RL], 36, 44, home(2, chain_half)).start()

    def late_reflected():
        V[RC] = V[R01] + mm(W[U01], mm(W[R23], V[G3]))
        message(V.at[RC], V.at[RL], 35, 44, home(3, chain_half)).start()

    def arrived():
        got(rows(R23, 0), 39)
        got(rows(R23, 1), 47)

    @pl.when(is_a1)
    def _():
        arrived()
        late, early = mm(W[Q01], W[R23]), mm(W[HQ], W[ROUT])
        late_value, early_value = V[T01], V[HT]
        for _ in range(3):
            late_value = V[T01] + mm(late, late_value)
            early_value = V[HT] + mm(early, early_value)
        V[G3] = late_value
        V[G2] = early_value
        stack_field()
        V[P1] = mm(W[POUT], early_value)
        step_field()
        late_reflected()
        early_reflected()

    @pl.when(is_b0)
    def _():
        V[G2] = bounced(mm(W[HQ], W[ROUT]), V[HT])
        V[P1] = mm(W[POUT], V[G2])
        step_field()
        arrived()
        V[G3] = bounced(mm(W[Q01], W[R23]), V[T01])
        stack_field()
        late_reflected()
        early_reflected()

    finals.append((is_hub, V.at[P1], 34))
    finals.append((is_hub, V.at[RB], 36))
    finals.append((is_hub, V.at[G3], 33))
    finals.append((is_hub, V.at[RC], 35))

    @pl.when(is_a3)
    def _():
        got(W.at[POUT], 40)
        W[T3] = mm(W[CT], W[POUT])

    @pl.when(is_last & (c == 1))
    def _():
        got(W.at[T3], 40)

    @pl.when(is_two)
    def _():
        got(V.at[PL], 41)
        V[TA] = mm(W[CT], V[PL])

    post(is_two, V.at[TA], V.at[ENT], 31, 45, 32 * (4 + chain_half) + residue + 1)
    post(is_two, V.at[TA], V.at[TL], 30, 43, home(2, chain_half))

    @pl.when(is_last)
    def _():
        got(V.at[GL], 42)
        V[TB] = mm(W[T3], V[GL])

    post(is_last & goes_on, V.at[TB], V.at[ENT], 38, 45, 32 * (6 + chain_half) + residue + 1)
    post(is_last, V.at[TB], V.at[TL], 37, 43, home(3, chain_half))

    @pl.when((y < 2) & ~is_first_home)
    def _():
        got(V.at[pl.ds(TL, 2)], 43)

    @pl.when(y >= 2)
    def _():
        got(V.at[TL], 43)
        got(V.at[RL], 44)

    through_copy = pltpu.make_async_copy(V.at[TL], through_out.at[0], local.at[3])
    reflected_copy = pltpu.make_async_copy(V.at[RL], reflected_out.at[0], local.at[4])
    through_copy.start()
    reflected_copy.start()

    @pl.when(me >= 1)
    def _():
        got(V.at[ENT], 45)

    @pl.when(me == 0)
    def _():
        V[ENT] = incident_ref[...]

    depth[...] = jnp.dot(maps_left[...], right(V[ENT]), preferred_element_type=F32).reshape(
        DEPTHS, M, INC
    )
    depth_copy = pltpu.make_async_copy(depth, depth_out.at[0], local.at[5])
    depth_copy.start()

    for part in (2, 3):
        for half in (0, 1):
            sent(piece(part, half), 2 * part + half)
    for condition, source, s in finals:
        @pl.when(condition)
        def _(source=source, s=s):
            sent(source, s)

    through_copy.wait()
    reflected_copy.wait()
    depth_copy.wait()


def results_kernel(through_ref, reflected_ref, depth_ref, through_out, reflected_out, depth_out,
                   held, inward, outward):
    pieces = [(through_ref.at[0], through_out.at[0]), (reflected_ref.at[0], reflected_out.at[0])]
    pieces += [(depth_ref.at[0, j], depth_out.at[0, j]) for j in range(DEPTHS)]
    arriving = [
        pltpu.make_async_copy(source, held.at[i], inward.at[i]) for i, (source, _) in enumerate(pieces)
    ]
    leaving = [
        pltpu.make_async_copy(held.at[i], target, outward.at[i]) for i, (_, target) in enumerate(pieces)
    ]
    for copy in arriving:
        copy.start()
    for copy, after in zip(arriving, leaving):
        copy.wait()
        after.start()
    for copy in leaving:
        copy.wait()


def per_device(front_reflect, front_through, back_reflect, back_through, depth_maps, incident):
    anywhere = pl.BlockSpec(memory_space=pl.ANY)
    results = (
        jax.ShapeDtypeStruct((1, M, INC), F32),
        jax.ShapeDtypeStruct((1, M, INC), F32),
        jax.ShapeDtypeStruct((1, DEPTHS, M, INC), F32),
    )
    made = pl.pallas_call(
        kernel,
        out_shape=results,
        in_specs=[anywhere] * 5 + [pl.BlockSpec(memory_space=pltpu.VMEM)],
        out_specs=(anywhere,) * 3,
        scratch_shapes=[
            pltpu.VMEM((BLOCKS, M, M), F32),
            pltpu.VMEM((VECS, M, INC), F32),
            pltpu.VMEM((DEPTHS, M, M), F32),
            pltpu.VMEM((DEPTHS * M, 3 * M), BF16),
            pltpu.VMEM((DEPTHS, M, INC), F32),
            pltpu.SemaphoreType.DMA((45,)),
            pltpu.SemaphoreType.DMA((49,)),
            pltpu.SemaphoreType.DMA((6,)),
        ],
        compiler_params=pltpu.CompilerParams(
            collective_id=0, has_side_effects=True, vmem_limit_bytes=60 * 2**20
        ),
        name="chains",
    )(front_reflect, front_through, back_reflect, back_through, depth_maps, incident)
    return pl.pallas_call(
        results_kernel,
        out_shape=results,
        in_specs=[anywhere] * 3,
        out_specs=(anywhere,) * 3,
        scratch_shapes=[
            pltpu.VMEM((2 + DEPTHS, M, INC), F32),
            pltpu.SemaphoreType.DMA((2 + DEPTHS,)),
            pltpu.SemaphoreType.DMA((2 + DEPTHS,)),
        ],
        compiler_params=pltpu.CompilerParams(vmem_limit_bytes=60 * 2**20),
        name="results",
    )(*made)


def solution(mesh):
    in_specs = (
        P("sec", None, None),
        P("sec", None, None),
        P("sec", None, None),
        P("sec", None, None),
        P("sec", None, None, None),
        P(),
    )
    out_specs = (P("sec", None, None), P("sec", None, None), P("sec", None, None, None))
    return jax.shard_map(
        per_device, mesh=mesh, in_specs=in_specs, out_specs=out_specs, check_vma=False
    )
```
